32 devices in a mesh: groups: 2 (over y), row: 4 (over x, core), col: 4 (over z).
Axes of the slice: x: 2, y: 2, z: 4, core: 2. Of those that a mesh axis runs over, the one named last changes fastest.
Arguments:
- sigma_sep: bfloat16 [30720, 15360], P(('groups', 'row'), 'col'), parts along dimension 0, may hold values from -3 to 3
- pattern_a: int32 [120], replicated, may hold values 0 or 1
- pattern_b: int32 [120], replicated, may hold values 0 or 1
- panel_a: bfloat16 [30720, 512], P(('groups', 'col'), 'row'), parts along dimension 0, may hold values from -0.09375 to 0.09375
- panel_b: bfloat16 [30720, 512], P(('groups', 'col'), 'row'), parts along dimension 0, may hold values from -0.09375 to 0.09375
- cross_b: float32 [1024, 512], P('groups'), parts along dimension 0, may hold values from -0.25 to 0.25
- dinv_a: float32 [1024, 512], P(('groups', 'col')), parts along dimension 0, may hold values from -6 to 6
- dinv_b: float32 [1024, 512], P(('groups', 'col')), parts along dimension 0, may hold values from -6 to 6
Outputs:
- sigma_ia: float32 [30720, 512], P(('groups', 'row'), 'col'), parts along dimension 0
- sigma_aa: float32 [1024, 512], P(('groups', 'col')), parts along dimension 0
- sigma_ib: float32 [30720, 512], P(('groups', 'row'), 'col'), parts along dimension 0
- sigma_ab: float32 [1024, 512], P(('groups', 'col'), 'row'), parts along dimension 0
- sigma_bb: float32 [1024, 512], P(('groups', 'col')), parts along dimension 0
The draws below stay inside these ranges and needn't reach their ends.
There are 2 independent parts, one for each index of `groups`. The reference program is written for one: setup_inputs(seed, part) draws one part's arguments, and reference() takes and returns one part's arrays. A program takes and returns all parts, laid end to end along the dimension named above; an argument that names none is the same for every part. Nothing has to cross between parts.
All inputs are finite; a program needn't handle non-finite values.
Results may differ from the reference program's by a relative error of at most 0.0003.
Values may be sent and summed in bfloat16 or wider, within the bound.
No kernel may reach another device: no remote copies, remote signals or barrier semaphores. Data moves between devices by JAX's collectives and lax.ppermute only.
A program may use at most 192 MiB of HBM per device.

```python
import jax
import jax.numpy as jnp
from jax import lax

BLK = 128
S = 15360
P_SIZE = 512
SB = 120


def set_ends(values, key, smallest, high):
    longest = values.shape.index(max(values.shape))
    spots = []
    for shift in (0, 1):
        where = [jax.random.randint(jax.random.fold_in(key, axis), (), 0, length) for axis, length in enumerate(values.shape)]
        where[longest] = (where[longest] + shift) % values.shape[longest]
        spots.append(tuple(where))
    return values.at[spots[0]].set(smallest).at[spots[1]].set(high)


def level_of(key, shape, split, low, high):
    level = 1.0
    for dim, blocks in split:
        heights = jax.random.uniform(jax.random.fold_in(jax.random.fold_in(key, 6), dim), (blocks,), jnp.float32, low / len(split), high / len(split))
        level = level * jnp.repeat(jnp.exp(heights), shape[dim] // blocks).reshape((-1,) + (1,) * (len(shape) - 1 - dim))
    return level


def centred(own_key, dims, deviation, bound, pieces=(), dtype=jnp.bfloat16):
    gain = level_of(own_key, dims, pieces, -0.22, 0.18) if pieces else 1.0
    result = jax.random.normal(own_key, dims, jnp.float32) * deviation * gain
    return jnp.minimum(jnp.maximum(result, -bound), bound).astype(dtype)


def setup_inputs(seed: int = 0, part: int = 0) -> dict:
    splits = jax.random.split(jax.random.key(seed), 9)
    part_splits = jax.random.split(jax.random.fold_in(splits[8], part), 9)
    sigma_sep = centred(part_splits[0], (S, S), 0.5, 3.0, ((0, 4), (1, 4)))
    pattern_a = set_ends((jax.random.randint(splits[1], (SB,), 0, 4) < 3).astype(jnp.int32), jax.random.fold_in(splits[1], 1), 0, 1)
    pattern_b = set_ends((jax.random.randint(splits[2], (SB,), 0, 4) < 3).astype(jnp.int32), jax.random.fold_in(splits[2], 1), 0, 1)
    panel_a = centred(part_splits[3], (S, P_SIZE), (S // 4) ** -0.5, 0.09375, ((0, 4), (1, 4)))
    panel_b = centred(part_splits[4], (S, P_SIZE), (S // 4) ** -0.5, 0.09375, ((0, 4), (1, 4)))
    cross_b = centred(part_splits[5], (P_SIZE, P_SIZE), P_SIZE ** -0.5, 0.25, (), jnp.float32)
    dinv_a = centred(part_splits[6], (P_SIZE, P_SIZE), 1.0, 6.0, ((0, 4),), jnp.float32)
    dinv_b = centred(part_splits[7], (P_SIZE, P_SIZE), 1.0, 6.0, ((0, 4),), jnp.float32)
    return {"sigma_sep": sigma_sep, "pattern_a": pattern_a, "pattern_b": pattern_b, "panel_a": panel_a, "panel_b": panel_b, "cross_b": cross_b, "dinv_a": dinv_a, "dinv_b": dinv_b}


def expand_mask(pattern):
    return jnp.repeat(pattern, BLK).astype(jnp.float32)[:, None]


def product(left, right):
    return jnp.dot(left, right, precision=lax.Precision.HIGHEST, preferred_element_type=jnp.float32)


def reference(sigma_sep, pattern_a, pattern_b, panel_a, panel_b, cross_b, dinv_a, dinv_b):
    mask_a = expand_mask(pattern_a)
    mask_b = expand_mask(pattern_a * pattern_b)
    masked_a = (mask_a * panel_a.astype(jnp.float32)).astype(jnp.bfloat16)
    masked_b = (mask_b * panel_b.astype(jnp.float32)).astype(jnp.bfloat16)
    image_a = jnp.dot(sigma_sep, masked_a, preferred_element_type=jnp.float32)
    sigma_ia = -mask_a * image_a
    sigma_aa = dinv_a + product(image_a.T, masked_a.astype(jnp.float32))
    image_b = jnp.dot(sigma_sep, masked_b, preferred_element_type=jnp.float32) + product(sigma_ia, cross_b)
    sigma_ib = -mask_b * image_b
    image_ab = product(sigma_ia.T, masked_b.astype(jnp.float32)) + product(sigma_aa, cross_b)
    sigma_ab = -image_ab
    sigma_bb = dinv_b + product(masked_b.astype(jnp.float32).T, image_b) + product(cross_b.T, image_ab)
    return (sigma_ia, sigma_aa, sigma_ib, sigma_ab, sigma_bb)
```

```python
import functools

import jax
import jax.numpy as jnp
from jax import lax
from jax.experimental import pallas as pl
from jax.experimental.pallas import tpu as pltpu
from jax.sharding import PartitionSpec as P

BLK = 128
TOP = 32704.0
STEPS = 64.0
LN2 = 0.6931471805599453
ROUND = 1.5 * 2.0**23
TAIL = 16
VMEM = 40 * 2**20

PIECE = 5
DEPTH_STEPS = 3


def code_of(values):
    top = jnp.max(jnp.abs(values), axis=0, keepdims=True)
    return jnp.ceil(jnp.log(jnp.maximum(top, 1e-30)) * (STEPS / LN2))


def scale_of(code):
    return jnp.exp(code * (LN2 / STEPS))


def coded(values, code):
    values = (values * (TOP / scale_of(code)) + ROUND) - ROUND
    return values.astype(jnp.int32).astype(jnp.int16)


def pick(table, row):
    rows = lax.broadcasted_iota(jnp.int32, table.shape, 0)
    return jnp.sum(jnp.where(rows == row, table, 0.0), axis=0, keepdims=True)


def put(table_ref, row, value):
    rows = lax.broadcasted_iota(jnp.int32, table_ref.shape, 0)
    table_ref[...] = jnp.where(rows == row, value, table_ref[...])


def decoded(message, block):
    table = message[PIECE * BLK :, :].astype(jnp.int32).astype(jnp.float32)
    values = message[block * BLK : (block + 1) * BLK, :].astype(jnp.int32).astype(jnp.float32)
    return values * (scale_of(pick(table, block)) * (1.0 / TOP))


def encode(block, values, codes, outs):
    code = code_of(values)
    values = coded(values, code)
    columns = values.shape[1] // len(outs)
    for part, out in enumerate(outs):
        out[block * BLK : (block + 1) * BLK, :] = values[:, part * columns : (part + 1) * columns]
    rows = lax.broadcasted_iota(jnp.int32, codes.shape, 0)
    return jnp.where(rows == block, code, codes)


def close(codes, outs):
    codes = codes.astype(jnp.int32).astype(jnp.int16)
    columns = codes.shape[1] // len(outs)
    for part, out in enumerate(outs):
        out[PIECE * BLK :, :] = codes[:, part * columns : (part + 1) * columns]


def split(values):
    high = values.astype(jnp.bfloat16)
    return high, (values - high.astype(jnp.float32)).astype(jnp.bfloat16)


def over_rows(left, right):
    return lax.dot_general(
        left, right, (((0,), (0,)), ((), ())), preferred_element_type=jnp.float32
    )


def dot(left, right):
    return jnp.dot(left, right, preferred_element_type=jnp.float32)


def whole(shape):
    return pl.BlockSpec(shape, lambda i, *_: (0,) * len(shape))


def params():
    return pltpu.CompilerParams(vmem_limit_bytes=VMEM)


FIELDS = 2 + PIECE
ENDS, PARITY, OWN = range(3)
SPOTS = 3


def here():
    return pl.BlockSpec(memory_space=pl.ANY)


def far_off():
    return pl.BlockSpec(memory_space=pltpu.HBM)


def join_kernel(spot, mask, blocks, table, mine_ref, theirs_ref, *refs):
    out_ref = refs[-1]
    even = table[spot + PARITY] == 0
    for block in range(blocks):
        rows = slice(block * BLK, (block + 1) * BLK)
        mine, theirs = mine_ref[rows, :], theirs_ref[rows, :]
        on = table[mask + pl.program_id(0) * blocks + block] == 1
        zero = jnp.zeros_like(mine)
        out_ref[rows, :BLK] = jnp.where(on, jnp.where(even, mine, theirs), zero)
        out_ref[rows, BLK:] = jnp.where(on, jnp.where(even, theirs, mine), zero)


def join(spot, mask, table, mine, theirs, after):
    rows = mine.shape[0]
    blocks = rows // (BLK * DEPTH_STEPS)
    block = pl.BlockSpec((blocks * BLK, BLK), lambda i, *_: (i, 0))
    return pl.pallas_call(
        functools.partial(join_kernel, spot, mask, blocks),
        grid_spec=pltpu.PrefetchScalarGridSpec(
            num_scalar_prefetch=1,
            grid=(DEPTH_STEPS,),
            in_specs=[block, block] + [here()] * len(after),
            out_specs=pl.BlockSpec((blocks * BLK, 2 * BLK), lambda i, *_: (i, 0)),
        ),
        out_shape=pltpu.HBM((rows, 2 * BLK), mine.dtype),
        compiler_params=params(),
        cost_estimate=pl.CostEstimate(
            flops=rows * BLK, bytes_accessed=8 * rows * BLK, transcendentals=0
        ),
        name="join",
    )(table, mine, theirs, *after)


def pass_kernel(in_ref, *refs):
    refs[-1][...] = in_ref[...]


def passed(value, after):
    block = pl.BlockSpec(value.shape, lambda i: (0,) * value.ndim)
    return pl.pallas_call(
        pass_kernel,
        grid=(1,),
        in_specs=[block] + [here()] * len(after),
        out_specs=block,
        out_shape=jax.ShapeDtypeStruct(value.shape, value.dtype),
        compiler_params=params(),
        cost_estimate=pl.CostEstimate(
            flops=value.size, bytes_accessed=4 * value.size, transcendentals=0
        ),
        name="passed",
    )(value, *after)


def slot_kernel(slot, spot, sections, gots, end, waits, aliases, table, *refs):
    refs = list(refs)

    def take(count):
        taken = refs[:count]
        del refs[:count]
        return taken

    (sigma,) = take(1)
    panels = take(len(sections))
    got_refs = take(gots)
    if end == "b":
        terms = take(4)
        cross_high, cross_low = take(2)
        rows_0, rows_1 = take(PIECE), take(PIECE)
        (total_in,) = take(1)
    take(waits + aliases)
    (msg_ref,) = take(1)
    if end == "a":
        high_ref, low_ref = take(2)
    if end:
        slice_refs = [ref.at[0] for ref in take(2)]
    if end == "b":
        (total_ref,) = take(1)
    acc, left, rhs, sems = take(4)
    valid = table[slot * FIELDS] == 1
    ends = table[spot + ENDS] == 1
    part = rhs.shape[0] // DEPTH_STEPS

    def panel_copy(panel, which):
        span = pl.ds(which * part, part)
        return pltpu.make_async_copy(panel.at[span, :], rhs.at[span, :], sems.at[which, PIECE])

    def sigma_copy(block, which):
        first = pl.multiple_of(table[slot * FIELDS + 2 + block] * BLK, BLK)
        span = pl.ds(which * part, part)
        return pltpu.make_async_copy(
            sigma.at[pl.ds(first, BLK), span],
            left.at[pl.ds(block * BLK, BLK), span],
            sems.at[which, block],
        )

    @pl.when(valid)
    def _():
        for which in range(DEPTH_STEPS):
            for section, panel in zip(sections, panels):

                @pl.when(table[slot * FIELDS + 1] == section)
                def _():
                    panel_copy(panel, which).start()

            for block in range(PIECE):
                sigma_copy(block, which).start()
        for which in range(DEPTH_STEPS):
            panel_copy(panels[0], which).wait()
            for block in range(PIECE):
                sigma_copy(block, which).wait()
            span = slice(which * part, (which + 1) * part)
            values = dot(left[:, span], rhs[span, :])
            if which:
                acc[...] += values
            else:
                acc[...] = values

    def values_of(block):
        values = acc[block * BLK : (block + 1) * BLK, :]
        for got_ref in got_refs:
            values = values + decoded(got_ref, block)
        return values

    blank = jnp.zeros((TAIL, acc.shape[1]), jnp.float32)

    @pl.when(valid & jnp.logical_not(ends))
    def _():
        codes = blank
        for block in range(PIECE):
            codes = encode(block, values_of(block), codes, [msg_ref])
        close(codes, [msg_ref])

    if end == "a":

        @pl.when(ends)
        def _():
            codes = blank
            for block in range(PIECE):
                values = values_of(block)
                rows = slice(block * BLK, (block + 1) * BLK)
                high_ref[rows, :], low_ref[rows, :] = split(values)
                codes = encode(block, values, codes, slice_refs)
            close(codes, slice_refs)

    if end == "b":

        @pl.when(ends)
        def _():
            high = jnp.concatenate([terms[0][...], terms[2][...]], axis=1)
            low = jnp.concatenate([terms[1][...], terms[3][...]], axis=1)
            acc[...] -= (
                dot(high, cross_high[...])
                + dot(high, cross_low[...])
                + dot(low, cross_high[...])
            )
            codes = blank
            for block in range(PIECE):
                values = values_of(block)
                acc[block * BLK : (block + 1) * BLK, :] = values
                codes = encode(block, values, codes, slice_refs)
            close(codes, slice_refs)
            high, low = split(acc[...])
            rows = jnp.concatenate(
                [jnp.concatenate([x[...], y[...]], axis=1) for x, y in zip(rows_0, rows_1)],
                axis=0,
            )
            total_ref[...] = total_in[...] + (over_rows(rows, high) + over_rows(rows, low))


def run_slot(slot, spot, table, sigma, panels, gots, end, extra, after, buffers, spots):
    depth = sigma.shape[1]
    width = next(iter(panels.values())).shape[1]
    rows = PIECE * BLK
    base = slot * FIELDS

    def panel_row(which):
        return lambda i, table: (table[base + 2 + which], 0)

    in_specs = [far_off()] * (1 + len(panels))
    operands = [sigma] + list(panels.values())
    message = (rows + TAIL, width)
    in_specs += [whole(message)] * len(gots)
    operands += gots
    out_specs = [whole(message)]
    out_shape = [jax.ShapeDtypeStruct(message, jnp.int16)]
    if end:
        piece, pieces, place_in, places = spots
    if end == "a":
        out_specs += [pl.BlockSpec((rows, width), lambda i, *_: (piece, 0))] * 2
        out_shape += [pltpu.HBM((pieces * rows, width), jnp.bfloat16)] * 2
    if end:
        slice_message = (1, rows + TAIL, width // 2)
        out_specs += [pl.BlockSpec(slice_message, lambda i, *_: (place_in, 0, 0))] * 2
        out_shape += [pltpu.HBM((places,) + slice_message[1:], jnp.int16)] * 2
    if end == "b":
        terms, cross, both, total = extra
        in_specs += [pl.BlockSpec((rows, width), lambda i, *_: (piece, 0))] * 4
        in_specs += [whole((2 * width, width))] * 2
        for _ in range(2):
            in_specs += [pl.BlockSpec((BLK, width), panel_row(which)) for which in range(PIECE)]
        in_specs.append(whole((2 * width, width)))
        operands += [*terms, *cross] + [both[0]] * PIECE + [both[1]] * PIECE + [total]
        out_specs.append(whole((2 * width, width)))
        out_shape.append(jax.ShapeDtypeStruct((2 * width, width), jnp.float32))
    in_specs += [here()] * len(after)
    operands += after
    aliases = {}
    count = 0
    for which, buffer in enumerate(buffers):
        if buffer is not None:
            aliases[1 + len(operands)] = 1 + which
            in_specs.append(far_off())
            operands.append(buffer)
            count += 1
    return pl.pallas_call(
        functools.partial(
            slot_kernel, slot, spot, tuple(panels), len(gots), end, len(after), count
        ),
        grid_spec=pltpu.PrefetchScalarGridSpec(
            num_scalar_prefetch=1,
            grid=(1,),
            in_specs=in_specs,
            out_specs=out_specs,
            scratch_shapes=[
                pltpu.VMEM((rows, width), jnp.float32),
                pltpu.VMEM((rows, depth), jnp.bfloat16),
                pltpu.VMEM((depth, width), jnp.bfloat16),
                pltpu.SemaphoreType.DMA((DEPTH_STEPS, PIECE + 1)),
            ],
        ),
        out_shape=out_shape,
        input_output_aliases=aliases,
        compiler_params=params(),
        cost_estimate=pl.CostEstimate(
            flops=rows * width,
            bytes_accessed=rows * width,
            transcendentals=0,
        ),
        name="slot",
    )(table, *operands)


def square_kernel(spot, table, *refs):
    high_ref, low_ref, *panels, in_ref, out_ref = refs

    @pl.when(table[spot + ENDS] == 1)
    def _():
        @pl.when(pl.program_id(0) == 0)
        def _():
            out_ref[...] = in_ref[...]

        rows = jnp.concatenate(
            [
                jnp.concatenate([ref[...] for ref in panels[first : first + PIECE]], axis=0)
                for first in range(0, len(panels), PIECE)
            ],
            axis=1,
        )
        out_ref[...] += over_rows(high_ref[...], rows) + over_rows(low_ref[...], rows)


def square_sums(spot, order, table, first, count, terms, panels, total):
    width = terms[0].shape[1]
    rows = PIECE * BLK
    term = pl.BlockSpec((rows, width), lambda i, *_: (first + i, 0))

    def panel_row(which):
        return lambda i, table: (table[order + (first + i) * PIECE + which], 0)

    shape = (width, len(panels) * width)
    blocks = [pl.BlockSpec((BLK, width), panel_row(which)) for which in range(PIECE)]
    return pl.pallas_call(
        functools.partial(square_kernel, spot),
        grid_spec=pltpu.PrefetchScalarGridSpec(
            num_scalar_prefetch=1,
            grid=(count,),
            in_specs=[term] * 2 + blocks * len(panels) + [whole(shape)],
            out_specs=whole(shape),
        ),
        out_shape=jax.ShapeDtypeStruct(shape, jnp.float32),
        compiler_params=params(),
        cost_estimate=pl.CostEstimate(
            flops=16 * count * rows * width * width,
            bytes_accessed=12 * count * rows * width + 32 * width * width,
            transcendentals=0,
        ),
        name="square_sums",
    )(table, *terms, *[panel for panel in panels for _ in range(PIECE)], total)


def place_kernel(spot, on, order, pieces, parts, table, *refs):
    arrays = refs[: 2 * len(parts)]
    out_ref, held, sem = refs[2 * len(parts) :]
    own = table[spot + OWN]
    ends = table[spot + ENDS] == 1
    for which, (v, start, count) in enumerate(parts):
        for side, wanted in ((0, ends), (1, jnp.logical_not(ends))):

            @pl.when((own == v) & wanted)
            def _():
                source = arrays[2 * which + side]
                copy = pltpu.make_async_copy(source, held.at[pl.ds(start, count)], sem)
                copy.start()
                copy.wait()

    out_ref[...] = jnp.zeros_like(out_ref)

    @pl.loop(0, pieces)
    def _(piece):
        message = held.at[piece]
        for block in range(PIECE):
            which = piece * PIECE + block
            first = pl.multiple_of(table[order + which] * BLK, BLK)
            values = jnp.where(table[on + which] == 1, -decoded(message, block), 0.0)
            out_ref[pl.ds(first, BLK), :] = values


def place(spot, on, order, table, pieces, row_count, parts):
    message = parts[0][2].shape[1:]
    ranges = tuple((v, start, mine.shape[0]) for v, start, mine, _ in parts)
    arrays = [array for part in parts for array in part[2:]]
    return pl.pallas_call(
        functools.partial(place_kernel, spot, on, order, pieces, ranges),
        grid_spec=pltpu.PrefetchScalarGridSpec(
            num_scalar_prefetch=1,
            grid=(1,),
            in_specs=[far_off()] * len(arrays),
            out_specs=whole((row_count, BLK)),
            scratch_shapes=[
                pltpu.VMEM((pieces,) + message, jnp.int16),
                pltpu.SemaphoreType.DMA(()),
            ],
        ),
        out_shape=jax.ShapeDtypeStruct((row_count, BLK), jnp.float32),
        compiler_params=params(),
        cost_estimate=pl.CostEstimate(
            flops=20 * row_count * BLK,
            bytes_accessed=6 * row_count * BLK,
            transcendentals=0,
        ),
        name="place",
    )(table, *arrays)


def product(left, right):
    return jnp.dot(left, right, precision=lax.Precision.HIGHEST, preferred_element_type=jnp.float32)


def plan(
    pieces_a, pieces_b,
    sigma_sep, pattern_a, pattern_b, panel_a, panel_b, cross_b, dinv_a, dinv_b,
):
    rows_n = lax.axis_size("row")
    cols_n = lax.axis_size("col")
    row = lax.axis_index("row")
    col = lax.axis_index("col")
    local_rows, local_cols = sigma_sep.shape
    ratio = rows_n // cols_n
    row_blocks = local_rows // BLK
    col_blocks = local_cols // BLK
    width = panel_a.shape[1] * rows_n
    half_width = width // 2
    slices = width // BLK
    pair = row // 2
    diag = row // ratio
    on_diag = col == diag

    def at(r, c):
        return r * cols_n + c

    def home(r, v):
        return (v + 2 * (r // 2)) % slices

    ends = [(r, r // ratio) for r in range(rows_n)]
    spread = [
        [(at(r, d), at(r, home(r, v))) for r, d in ends if home(r, v) != d]
        for v in range(slices)
    ]
    own_v = (col + 2 * pair) % slices

    def path(d):
        if 2 * d < cols_n:
            return list(range(d)) + list(range(cols_n - 1, d - 1, -1))
        return list(range(cols_n - 1, d, -1)) + list(range(d + 1))

    def send(value, pairs):
        return lax.ppermute(value, ("row", "col"), pairs)

    core_swap = [(r, r ^ 1) for r in range(rows_n)]
    chip_swap = [(r, (r + 2) % rows_n) for r in range(rows_n)]
    cross_swap = [(r, (r + 2) % rows_n ^ 1) for r in range(rows_n)]

    core_a = lax.ppermute(panel_a, "row", core_swap)
    chip_a = lax.ppermute(panel_a, "row", chip_swap)
    both_a = lax.ppermute(panel_a, "row", cross_swap)

    lengths = (pieces_a, pieces_a, pieces_b, pieces_b)
    starts = [sum(lengths[:section]) for section in range(4)]
    count = sum(lengths)
    far = cols_n - 1
    slots = count + 2 * far
    low = jnp.where(col < diag, col, diag + cols_n - 1 - col)
    high = jnp.where(col > diag, cols_n - 1 - col, cols_n - 1 - diag + col)
    delay = 2 * jnp.where(2 * diag < cols_n, low, high)
    at_slot = jnp.arange(slots, dtype=jnp.int32) - delay
    valid = (at_slot >= 0) & (at_slot < count)
    at_slot = jnp.clip(at_slot, 0, count - 1)
    section_at = sum((at_slot >= start).astype(jnp.int32) for start in starts[1:])
    piece_at = at_slot - sum(
        jnp.where(section_at == section, start, 0) for section, start in enumerate(starts)
    )
    both = pattern_a * pattern_b
    masks = [
        lax.dynamic_slice_in_dim(pattern, index * length, length, 0)
        for index, length in ((col, col_blocks), (row, row_blocks))
        for pattern in (pattern_a, both)
    ]
    numbers = jnp.arange(row_blocks, dtype=jnp.int32)
    rank = (2 - masks[2] - masks[3]) * row_blocks + numbers
    place_of = jnp.sum((rank[None, :] < rank[:, None]).astype(jnp.int32), axis=1)
    is_at = place_of[None, :] == numbers[:, None]
    order = jnp.sum(jnp.where(is_at, numbers[None, :], 0), axis=1)
    rows_on = [jnp.sum(jnp.where(is_at, mask[None, :], 0), axis=1) for mask in masks[2:]]
    spots = piece_at[:, None] * PIECE + jnp.arange(PIECE, dtype=jnp.int32)[None, :]
    blocks = jnp.sum(
        jnp.where(spots[:, :, None] == numbers[None, None, :], order[None, None, :], 0), axis=2
    )
    table = jnp.concatenate(
        [valid.astype(jnp.int32)[:, None], section_at[:, None], blocks], axis=1
    ).reshape(-1)
    spot = slots * FIELDS
    small = jnp.stack([on_diag.astype(jnp.int32), row % 2, own_v])
    table = jnp.concatenate([table, small, *masks[:2], *rows_on, order])
    cols_a = spot + SPOTS
    cols_b = cols_a + col_blocks
    rows_a = cols_b + col_blocks
    rows_b = rows_a + row_blocks
    order_at = rows_b + row_blocks

    swapped = pair % 2 == 1

    def turn(value, axis):
        return jnp.where(swapped, jnp.roll(value, half_width, axis), value)

    cross_v = turn(turn(cross_b, 0), 1)
    cross_high = lax.reduce_precision(cross_v, 8, 7)
    cross_low = (cross_v - cross_high).astype(jnp.bfloat16)
    cross_high = cross_high.astype(jnp.bfloat16)

    def inward(slot):
        pairs = []
        for r, d in ends:
            line = path(d)
            for stop, (c, after) in enumerate(zip(line, line[1:])):
                if 0 <= slot - 2 * stop < count:
                    pairs.append((at(r, c), at(r, after)))
        return pairs

    def to_columns(value):
        total = None
        for v, pairs in enumerate(spread):
            mine = value[v * BLK : (v + 1) * BLK]
            got = jnp.where(on_diag & (own_v == v), mine, send(mine, pairs))
            total = got if total is None else total + got
        return total

    def over_cores(total):
        return total + lax.ppermute(total, "row", core_swap)

    def over_row(total):
        total = over_cores(total)
        return total + lax.ppermute(total, "row", chip_swap)

    def parts_of(length, last):
        parts = []
        first = 0
        while first < length:
            size = min(3, length - first)
            if last and length - first <= 3:
                size = min(2, max(1, length - first - 1))
            parts.append((first, size))
            first += size
        return parts

    batches = [parts_of(length, section == 3) for section, length in enumerate(lengths)]
    panels = {0: join(spot, cols_a, table, panel_a, core_a, [])}
    arrived = {}
    terms = {}
    slice_parts = ([], [])
    squares = [jnp.zeros((half_width, 2 * width), jnp.float32)] * 2
    totals = [jnp.zeros((width, half_width), jnp.float32)] * 2
    waiting = {}
    message = None
    end_a = 2 * far + 2 * pieces_a - 1
    middle = pieces_a // 2

    def add_squares(half, first, length):
        squares[half] = square_sums(
            spot, order_at, table, first, length, terms[half], list(panels.values()), squares[half]
        )

    for slot in range(slots):
        if slot == 2:
            later_b = passed(panel_b, [message])
            core_b = lax.ppermute(later_b, "row", core_swap)
            chip_b = lax.ppermute(later_b, "row", chip_swap)
            both_b = lax.ppermute(later_b, "row", cross_swap)
        if slot == starts[1] - 1:
            panels[1] = join(spot, cols_a, table, chip_a, both_a, [message])
        if slot == starts[2] - 2:
            panels[2] = join(spot, cols_b, table, later_b, core_b, [message])
        if slot == starts[2] - 1:
            panels[3] = join(spot, cols_b, table, chip_b, both_b, [message])
        gots = arrived.pop(slot - 2, [])
        ended = slot - 2 * far
        end = ""
        if ended >= 0:
            section = sum(ended >= start for start in starts[1:])
            piece = ended - starts[section]
            half = section % 2
            end = "ab"[section // 2]
        extra = None
        buffers = []
        places = None
        if end:
            batch = next(b for b in batches[section] if b[0] <= piece < b[0] + b[1])
            places = (piece, lengths[section], piece - batch[0], batch[1])
            if end == "a":
                buffers += terms.get(half, [None, None])
            buffers += slice_bufs if piece > batch[0] else [None, None]
        if end == "b":
            cols = slice(half * half_width, (half + 1) * half_width)
            extra = (
                terms[0] + terms[1],
                (cross_high[:, cols], cross_low[:, cols]),
                (panels[2], panels[3]),
                totals[half],
            )
        first = sum(max(0, ended) >= start for start in starts[1:])
        final = sum(slot >= start for start in starts[1:])
        after = [] if message is None else [message]
        after += waiting.pop(slot, [])
        outs = run_slot(
            slot,
            spot,
            table,
            sigma_sep,
            {section: panels[section] for section in range(first, final + 1)},
            gots,
            end,
            extra,
            after,
            buffers,
            places,
        )
        message = outs[0]
        if slot < slots - 2:
            arrived[slot] = [send(message, inward(slot))]
        if end == "a":
            terms[half] = list(outs[1:3])
        if end == "b":
            totals[half] = outs[-1]
        if end:
            start = 3 if end == "a" else 1
            slice_bufs = list(outs[start : start + 2])
            if piece == batch[0] + batch[1] - 1:
                parts = slice_parts[section // 2]
                for part in range(2):
                    got = send(slice_bufs[part], spread[2 * half + part])
                    parts.append((2 * half + part, batch[0], slice_bufs[part], got))
                    waiting.setdefault(slot + 7, []).append(got)
        if slot == end_a - 2:
            add_squares(0, 0, middle)
        if slot == end_a - 1:
            add_squares(0, middle, pieces_a - middle)
        if slot == end_a:
            add_squares(1, 0, pieces_a)
            whole_a = jnp.concatenate(squares, axis=0)
            whole_a = jnp.concatenate([turn(whole_a[:, :width], 1), turn(whole_a[:, width:], 1)], 1)
            sums = to_columns(whole_a)
        if slot == end_a + pieces_b - 1:
            sums = over_row(passed(sums, [message]))
            sigma_aa = dinv_a + sums[:, :width]
            image_ab = product(sigma_aa, cross_b) - sums[:, width:]
            own_ab = lax.dynamic_slice_in_dim(image_ab, row * BLK, BLK, 1)
            cross_own = lax.dynamic_slice_in_dim(cross_b, col * BLK, BLK, 1)
        if slot == end_a + pieces_b:
            share = to_columns(totals[0])
        if slot == end_a + min(7, 2 * pieces_b - 1):
            sigma_ia = place(
                spot, rows_a, order_at, table, pieces_a, local_rows, slice_parts[0]
            )
            waiting.setdefault(slot + 2, []).append(sigma_ia)
        if slot == end_a + pieces_b + 2:
            own_ab = passed(own_ab, [message])
            cross_ab = jnp.zeros((BLK, BLK), jnp.float32)
            for shift in range(cols_n):
                pairs = [(c, (c + shift) % cols_n) for c in range(cols_n)]
                there = lax.ppermute(own_ab, "col", pairs) if shift else own_ab
                source = (col + cols_n - shift) % cols_n
                left = lax.dynamic_slice_in_dim(cross_own, source * BLK, BLK, 0)
                cross_ab = cross_ab + product(left.T, there)
            sigma_ab = -own_ab
            blank = jnp.zeros((BLK, half_width), jnp.float32)
            share = turn(jnp.concatenate([share, blank], axis=1), 1)
            blank = jnp.zeros((BLK, width), jnp.float32)
            share = share + lax.dynamic_update_slice_in_dim(blank, cross_ab, row * BLK, 1)
            share = dinv_b + over_row(share)
    rest = over_cores(to_columns(totals[1]))
    other = lax.ppermute(rest, "row", chip_swap)
    sigma_bb = share + turn(jnp.concatenate([other, rest], axis=1), 1)
    sigma_ib = place(spot, rows_b, order_at, table, pieces_b, local_rows, slice_parts[1])
    return (sigma_ia, sigma_aa, sigma_ib, sigma_ab, sigma_bb)


PLANS = ((6, 6),)


def per_device(sigma_sep, pattern_a, pattern_b, panel_a, panel_b, cross_b, dinv_a, dinv_b):
    bands = lax.axis_size("row")
    most_a = jnp.max(jnp.sum(pattern_a.reshape(bands, -1), axis=1))
    most_b = jnp.max(jnp.sum((pattern_a * pattern_b).reshape(bands, -1), axis=1))
    fits = [(most_a <= a * PIECE) & (most_b <= b * PIECE) for a, b in PLANS]
    which = jnp.argmax(jnp.stack(fits))
    return lax.switch(
        which,
        [functools.partial(plan, a, b) for a, b in PLANS],
        sigma_sep,
        pattern_a,
        pattern_b,
        panel_a,
        panel_b,
        cross_b,
        dinv_a,
        dinv_b,
    )


def broadcast(value, axis, root):
    mine = lax.axis_index(axis) == root
    return lax.psum(jnp.where(mine, value, jnp.zeros_like(value)), axis)


def block_mask(pattern, first_row, row_count):
    blocks = (first_row + jnp.arange(row_count, dtype=jnp.int32)) // BLK
    block_ids = jnp.arange(pattern.shape[0], dtype=jnp.int32)
    matches = (blocks[:, None] == block_ids[None, :]).astype(jnp.float32)
    return product(matches, pattern.astype(jnp.float32)[:, None])


def per_device_any(sigma_sep, pattern_a, pattern_b, panel_a, panel_b, cross_b, dinv_a, dinv_b):
    row_devices = lax.axis_size("row")
    col_devices = lax.axis_size("col")
    row_index = lax.axis_index("row")
    col_index = lax.axis_index("col")
    local_rows = sigma_sep.shape[0]
    local_cols = sigma_sep.shape[1]
    panel_width = panel_a.shape[1] * row_devices
    slice_width = panel_width // col_devices
    band_width = panel_width // row_devices
    row_ratio = row_devices // col_devices
    pattern_both = pattern_a * pattern_b
    masked_a = (
        panel_a.astype(jnp.float32) * block_mask(pattern_a, col_index * local_cols, local_cols)
    ).astype(jnp.bfloat16)
    masked_b = (
        panel_b.astype(jnp.float32) * block_mask(pattern_both, col_index * local_cols, local_cols)
    ).astype(jnp.bfloat16)
    mask_a_rows = block_mask(pattern_a, row_index * local_rows, local_rows)
    mask_b_rows = block_mask(pattern_both, row_index * local_rows, local_rows)
    source_col = row_index // row_ratio
    offset = row_index % row_ratio * local_rows

    def own_rows(gathered):
        return lax.dynamic_slice_in_dim(gathered, offset, local_rows, 0)

    full_a = lax.all_gather(masked_a, "row", axis=1, tiled=True)
    rows_a = broadcast(own_rows(full_a), "col", source_col)
    rows_a32 = rows_a.astype(jnp.float32)
    partial_a = jnp.dot(sigma_sep, full_a, preferred_element_type=jnp.float32)
    image_a = lax.psum_scatter(partial_a, "col", scatter_dimension=1, tiled=True)
    sigma_ia = -mask_a_rows * image_a
    quadratic_a = lax.psum(product(image_a.T, rows_a32), "row")
    sigma_aa = dinv_a + quadratic_a
    full_b = lax.all_gather(masked_b, "row", axis=1, tiled=True)
    rows_b = broadcast(own_rows(full_b), "col", source_col)
    rows_b32 = rows_b.astype(jnp.float32)
    cross_rows = lax.dynamic_slice_in_dim(cross_b, col_index * slice_width, slice_width, 0)
    cross_cols = lax.dynamic_slice_in_dim(cross_b, row_index * band_width, band_width, 1)
    partial_b = jnp.dot(sigma_sep, full_b, preferred_element_type=jnp.float32) + product(
        sigma_ia, cross_rows
    )
    image_b = lax.psum_scatter(partial_b, "col", scatter_dimension=1, tiled=True)
    sigma_ib = -mask_b_rows * image_b
    upper_part = lax.psum_scatter(
        product(sigma_ia.T, rows_b32), "row", scatter_dimension=1, tiled=True
    )
    image_ab = upper_part + product(sigma_aa, cross_cols)
    sigma_ab = -image_ab
    first_term = product(rows_b32.T, image_b)
    second_term = product(cross_rows.T, image_ab)
    blank = jnp.zeros((panel_width, panel_width), jnp.float32)
    placed = lax.dynamic_update_slice_in_dim(blank, first_term, col_index * slice_width, 1)
    placed = placed + lax.dynamic_update_slice_in_dim(blank, second_term, row_index * band_width, 1)
    share_b = lax.psum_scatter(placed, "col", scatter_dimension=0, tiled=True)
    total_bb = lax.psum(share_b, "row")
    sigma_bb = dinv_b + total_bb
    return (sigma_ia, sigma_aa, sigma_ib, sigma_ab, sigma_bb)


def tuned(mesh, sigma_sep, panel_a):
    rows_n, cols_n = mesh.shape["row"], mesh.shape["col"]
    rows = sigma_sep.shape[0] // (mesh.shape["groups"] * rows_n)
    cols = sigma_sep.shape[1] // cols_n
    return (
        rows_n == 4
        and cols_n == 4
        and panel_a.shape[1] == 4 * BLK
        and rows == BLK * PIECE * PLANS[-1][0]
        and cols % (DEPTH_STEPS * BLK) == 0
    )


def solution(mesh):
    placed = (
        P(("groups", "row"), "col"),
        P(),
        P(),
        P(("groups", "col"), "row"),
        P(("groups", "col"), "row"),
        P("groups", None),
        P(("groups", "col"), None),
        P(("groups", "col"), None),
    )
    out_placed = (
        P(("groups", "row"), "col"),
        P(("groups", "col"), None),
        P(("groups", "row"), "col"),
        P(("groups", "col"), "row"),
        P(("groups", "col"), None),
    )

    def run(sigma_sep, pattern_a, pattern_b, panel_a, panel_b, cross_b, dinv_a, dinv_b):
        body = per_device if tuned(mesh, sigma_sep, panel_a) else per_device_any
        return jax.shard_map(
            body, mesh=mesh, in_specs=placed, out_specs=out_placed, check_vma=False
        )(sigma_sep, pattern_a, pattern_b, panel_a, panel_b, cross_b, dinv_a, dinv_b)

    return run
```

```python
import functools

import jax
import jax.numpy as jnp
from jax import lax
from jax.experimental import pallas as pl
from jax.experimental.pallas import tpu as pltpu
from jax.sharding import PartitionSpec as P

BLK = 128
TOP = 32704.0
STEPS = 64.0
LN2 = 0.6931471805599453
ROUND = 1.5 * 2.0**23
TAIL = 16
VMEM = 40 * 2**20

PIECE = 10
DEPTH_STEPS = 3


def code_of(values):
    top = jnp.max(jnp.abs(values), axis=0, keepdims=True)
    return jnp.ceil(jnp.log(jnp.maximum(top, 1e-30)) * (STEPS / LN2))


def scale_of(code):
    return jnp.exp(code * (LN2 / STEPS))


def coded(values, code):
    values = (values * (TOP / scale_of(code)) + ROUND) - ROUND
    return values.astype(jnp.int32).astype(jnp.int16)


def pick(table, row):
    rows = lax.broadcasted_iota(jnp.int32, table.shape, 0)
    return jnp.sum(jnp.where(rows == row, table, 0.0), axis=0, keepdims=True)


def put(table_ref, row, value):
    rows = lax.broadcasted_iota(jnp.int32, table_ref.shape, 0)
    table_ref[...] = jnp.where(rows == row, value, table_ref[...])


def decoded(message, block):
    table = message[PIECE * BLK :, :].astype(jnp.int32).astype(jnp.float32)
    values = message[block * BLK : (block + 1) * BLK, :].astype(jnp.int32).astype(jnp.float32)
    return values * (scale_of(pick(table, block)) * (1.0 / TOP))


def encode(block, values, codes, outs):
    code = code_of(values)
    values = coded(values, code)
    columns = values.shape[1] // len(outs)
    for part, out in enumerate(outs):
        out[block * BLK : (block + 1) * BLK, :] = values[:, part * columns : (part + 1) * columns]
    rows = lax.broadcasted_iota(jnp.int32, codes.shape, 0)
    return jnp.where(rows == block, code, codes)


def close(codes, outs):
    codes = codes.astype(jnp.int32).astype(jnp.int16)
    columns = codes.shape[1] // len(outs)
    for part, out in enumerate(outs):
        out[PIECE * BLK :, :] = codes[:, part * columns : (part + 1) * columns]


def split(values):
    high = values.astype(jnp.bfloat16)
    return high, (values - high.astype(jnp.float32)).astype(jnp.bfloat16)


def over_rows(left, right):
    return lax.dot_general(
        left, right, (((0,), (0,)), ((), ())), preferred_element_type=jnp.float32
    )


def dot(left, right):
    return jnp.dot(left, right, preferred_element_type=jnp.float32)


def whole(shape):
    return pl.BlockSpec(shape, lambda i, *_: (0,) * len(shape))


def params():
    return pltpu.CompilerParams(vmem_limit_bytes=VMEM)


FIELDS = 2 + PIECE
ENDS, PARITY, OWN = range(3)
SPOTS = 3


def here():
    return pl.BlockSpec(memory_space=pl.ANY)


def far_off():
    return pl.BlockSpec(memory_space=pltpu.HBM)


def join_kernel(spot, mask, blocks, table, mine_ref, theirs_ref, *refs):
    out_ref = refs[-1]
    even = table[spot + PARITY] == 0
    for block in range(blocks):
        rows = slice(block * BLK, (block + 1) * BLK)
        mine, theirs = mine_ref[rows, :], theirs_ref[rows, :]
        on = table[mask + pl.program_id(0) * blocks + block] == 1
        zero = jnp.zeros_like(mine)
        out_ref[rows, :BLK] = jnp.where(on, jnp.where(even, mine, theirs), zero)
        out_ref[rows, BLK:] = jnp.where(on, jnp.where(even, theirs, mine), zero)


def join(spot, mask, table, mine, theirs, after):
    rows = mine.shape[0]
    blocks = rows // (BLK * DEPTH_STEPS)
    block = pl.BlockSpec((blocks * BLK, BLK), lambda i, *_: (i, 0))
    return pl.pallas_call(
        functools.partial(join_kernel, spot, mask, blocks),
        grid_spec=pltpu.PrefetchScalarGridSpec(
            num_scalar_prefetch=1,
            grid=(DEPTH_STEPS,),
            in_specs=[block, block] + [here()] * len(after),
            out_specs=pl.BlockSpec((blocks * BLK, 2 * BLK), lambda i, *_: (i, 0)),
        ),
        out_shape=pltpu.HBM((rows, 2 * BLK), mine.dtype),
        compiler_params=params(),
        cost_estimate=pl.CostEstimate(
            flops=rows * BLK, bytes_accessed=8 * rows * BLK, transcendentals=0
        ),
        name="join",
    )(table, mine, theirs, *after)


def pass_kernel(in_ref, *refs):
    refs[-1][...] = in_ref[...]


def passed(value, after):
    block = pl.BlockSpec(value.shape, lambda i: (0,) * value.ndim)
    return pl.pallas_call(
        pass_kernel,
        grid=(1,),
        in_specs=[block] + [here()] * len(after),
        out_specs=block,
        out_shape=jax.ShapeDtypeStruct(value.shape, value.dtype),
        compiler_params=params(),
        cost_estimate=pl.CostEstimate(
            flops=value.size, bytes_accessed=4 * value.size, transcendentals=0
        ),
        name="passed",
    )(value, *after)


def slot_kernel(slot, spot, sections, gots, end, waits, aliases, table, *refs):
    refs = list(refs)

    def take(count):
        taken = refs[:count]
        del refs[:count]
        return taken

    (sigma,) = take(1)
    panels = take(len(sections))
    got_refs = take(gots)
    if end == "b":
        terms = take(4)
        cross_high, cross_low = take(2)
        rows_0, rows_1 = take(PIECE), take(PIECE)
        (total_in,) = take(1)
    take(waits + aliases)
    (msg_ref,) = take(1)
    if end == "a":
        high_ref, low_ref = take(2)
    if end:
        slice_refs = [ref.at[0] for ref in take(2)]
    if end == "b":
        (total_ref,) = take(1)
    acc, left, rhs, sems = take(4)
    valid = table[slot * FIELDS] == 1
    ends = table[spot + ENDS] == 1
    part = rhs.shape[0] // DEPTH_STEPS

    def panel_copy(panel, which):
        span = pl.ds(which * part, part)
        return pltpu.make_async_copy(panel.at[span, :], rhs.at[span, :], sems.at[which, PIECE])

    def sigma_copy(block, which):
        first = pl.multiple_of(table[slot * FIELDS + 2 + block] * BLK, BLK)
        span = pl.ds(which * part, part)
        return pltpu.make_async_copy(
            sigma.at[pl.ds(first, BLK), span],
            left.at[pl.ds(block * BLK, BLK), span],
            sems.at[which, block],
        )

    @pl.when(valid)
    def _():
        for which in range(DEPTH_STEPS):
            for section, panel in zip(sections, panels):

                @pl.when(table[slot * FIELDS + 1] == section)
                def _():
                    panel_copy(panel, which).start()

            for block in range(PIECE):
                sigma_copy(block, which).start()
        for which in range(DEPTH_STEPS):
            panel_copy(panels[0], which).wait()
            for block in range(PIECE):
                sigma_copy(block, which).wait()
            span = slice(which * part, (which + 1) * part)
            values = dot(left[:, span], rhs[span, :])
            if which:
                acc[...] += values
            else:
                acc[...] = values

    def values_of(block):
        values = acc[block * BLK : (block + 1) * BLK, :]
        for got_ref in got_refs:
            values = values + decoded(got_ref, block)
        return values

    blank = jnp.zeros((TAIL, acc.shape[1]), jnp.float32)

    @pl.when(valid & jnp.logical_not(ends))
    def _():
        codes = blank
        for block in range(PIECE):
            codes = encode(block, values_of(block), codes, [msg_ref])
        close(codes, [msg_ref])

    if end == "a":

        @pl.when(ends)
        def _():
            codes = blank
            for block in range(PIECE):
                values = values_of(block)
                rows = slice(block * BLK, (block + 1) * BLK)
                high_ref[rows, :], low_ref[rows, :] = split(values)
                codes = encode(block, values, codes, slice_refs)
            close(codes, slice_refs)

    if end == "b":

        @pl.when(ends)
        def _():
            high = jnp.concatenate([terms[0][...], terms[2][...]], axis=1)
            low = jnp.concatenate([terms[1][...], terms[3][...]], axis=1)
            acc[...] -= (
                dot(high, cross_high[...])
                + dot(high, cross_low[...])
                + dot(low, cross_high[...])
            )
            codes = blank
            for block in range(PIECE):
                values = values_of(block)
                acc[block * BLK : (block + 1) * BLK, :] = values
                codes = encode(block, values, codes, slice_refs)
            close(codes, slice_refs)
            high, low = split(acc[...])
            rows = jnp.concatenate(
                [jnp.concatenate([x[...], y[...]], axis=1) for x, y in zip(rows_0, rows_1)],
                axis=0,
            )
            total_ref[...] = total_in[...] + (over_rows(rows, high) + over_rows(rows, low))


def run_slot(slot, spot, table, sigma, panels, gots, end, extra, after, buffers, spots):
    depth = sigma.shape[1]
    width = next(iter(panels.values())).shape[1]
    rows = PIECE * BLK
    base = slot * FIELDS

    def panel_row(which):
        return lambda i, table: (table[base + 2 + which], 0)

    in_specs = [far_off()] * (1 + len(panels))
    operands = [sigma] + list(panels.values())
    message = (rows + TAIL, width)
    in_specs += [whole(message)] * len(gots)
    operands += gots
    out_specs = [whole(message)]
    out_shape = [jax.ShapeDtypeStruct(message, jnp.int16)]
    if end:
        piece, pieces, place_in, places = spots
    if end == "a":
        out_specs += [pl.BlockSpec((rows, width), lambda i, *_: (piece, 0))] * 2
        out_shape += [pltpu.HBM((pieces * rows, width), jnp.bfloat16)] * 2
    if end:
        slice_message = (1, rows + TAIL, width // 2)
        out_specs += [pl.BlockSpec(slice_message, lambda i, *_: (place_in, 0, 0))] * 2
        out_shape += [pltpu.HBM((places,) + slice_message[1:], jnp.int16)] * 2
    if end == "b":
        terms, cross, both, total = extra
        in_specs += [pl.BlockSpec((rows, width), lambda i, *_: (piece, 0))] * 4
        in_specs += [whole((2 * width, width))] * 2
        for _ in range(2):
            in_specs += [pl.BlockSpec((BLK, width), panel_row(which)) for which in range(PIECE)]
        in_specs.append(whole((2 * width, width)))
        operands += [*terms, *cross] + [both[0]] * PIECE + [both[1]] * PIECE + [total]
        out_specs.append(whole((2 * width, width)))
        out_shape.append(jax.ShapeDtypeStruct((2 * width, width), jnp.float32))
    in_specs += [here()] * len(after)
    operands += after
    aliases = {}
    count = 0
    for which, buffer in enumerate(buffers):
        if buffer is not None:
            aliases[1 + len(operands)] = 1 + which
            in_specs.append(far_off())
            operands.append(buffer)
            count += 1
    return pl.pallas_call(
        functools.partial(
            slot_kernel, slot, spot, tuple(panels), len(gots), end, len(after), count
        ),
        grid_spec=pltpu.PrefetchScalarGridSpec(
            num_scalar_prefetch=1,
            grid=(1,),
            in_specs=in_specs,
            out_specs=out_specs,
            scratch_shapes=[
                pltpu.VMEM((rows, width), jnp.float32),
                pltpu.VMEM((rows, depth), jnp.bfloat16),
                pltpu.VMEM((depth, width), jnp.bfloat16),
                pltpu.SemaphoreType.DMA((DEPTH_STEPS, PIECE + 1)),
            ],
        ),
        out_shape=out_shape,
        input_output_aliases=aliases,
        compiler_params=params(),
        cost_estimate=pl.CostEstimate(
            flops=rows * width,
            bytes_accessed=rows * width,
            transcendentals=0,
        ),
        name="slot",
    )(table, *operands)


def square_kernel(spot, table, *refs):
    high_ref, low_ref, *panels, in_ref, out_ref = refs

    @pl.when(table[spot + ENDS] == 1)
    def _():
        @pl.when(pl.program_id(0) == 0)
        def _():
            out_ref[...] = in_ref[...]

        rows = jnp.concatenate(
            [
                jnp.concatenate([ref[...] for ref in panels[first : first + PIECE]], axis=0)
                for first in range(0, len(panels), PIECE)
            ],
            axis=1,
        )
        out_ref[...] += over_rows(high_ref[...], rows) + over_rows(low_ref[...], rows)


def square_sums(spot, order, table, first, count, terms, panels, total):
    width = terms[0].shape[1]
    rows = PIECE * BLK
    term = pl.BlockSpec((rows, width), lambda i, *_: (first + i, 0))

    def panel_row(which):
        return lambda i, table: (table[order + (first + i) * PIECE + which], 0)

    shape = (width, len(panels) * width)
    blocks = [pl.BlockSpec((BLK, width), panel_row(which)) for which in range(PIECE)]
    return pl.pallas_call(
        functools.partial(square_kernel, spot),
        grid_spec=pltpu.PrefetchScalarGridSpec(
            num_scalar_prefetch=1,
            grid=(count,),
            in_specs=[term] * 2 + blocks * len(panels) + [whole(shape)],
            out_specs=whole(shape),
        ),
        out_shape=jax.ShapeDtypeStruct(shape, jnp.float32),
        compiler_params=params(),
        cost_estimate=pl.CostEstimate(
            flops=16 * count * rows * width * width,
            bytes_accessed=12 * count * rows * width + 32 * width * width,
            transcendentals=0,
        ),
        name="square_sums",
    )(table, *terms, *[panel for panel in panels for _ in range(PIECE)], total)


def place_kernel(spot, on, order, pieces, parts, table, *refs):
    arrays = refs[: 2 * len(parts)]
    out_ref, held, sem = refs[2 * len(parts) :]
    own = table[spot + OWN]
    ends = table[spot + ENDS] == 1
    for which, (v, start, count) in enumerate(parts):
        for side, wanted in ((0, ends), (1, jnp.logical_not(ends))):

            @pl.when((own == v) & wanted)
            def _():
                source = arrays[2 * which + side]
                copy = pltpu.make_async_copy(source, held.at[pl.ds(start, count)], sem)
                copy.start()
                copy.wait()

    out_ref[...] = jnp.zeros_like(out_ref)

    @pl.loop(0, pieces)
    def _(piece):
        message = held.at[piece]
        for block in range(PIECE):
            which = piece * PIECE + block
            first = pl.multiple_of(table[order + which] * BLK, BLK)
            values = jnp.where(table[on + which] == 1, -decoded(message, block), 0.0)
            out_ref[pl.ds(first, BLK), :] = values


def place(spot, on, order, table, pieces, row_count, parts):
    message = parts[0][2].shape[1:]
    ranges = tuple((v, start, mine.shape[0]) for v, start, mine, _ in parts)
    arrays = [array for part in parts for array in part[2:]]
    return pl.pallas_call(
        functools.partial(place_kernel, spot, on, order, pieces, ranges),
        grid_spec=pltpu.PrefetchScalarGridSpec(
            num_scalar_prefetch=1,
            grid=(1,),
            in_specs=[far_off()] * len(arrays),
            out_specs=whole((row_count, BLK)),
            scratch_shapes=[
                pltpu.VMEM((pieces,) + message, jnp.int16),
                pltpu.SemaphoreType.DMA(()),
            ],
        ),
        out_shape=jax.ShapeDtypeStruct((row_count, BLK), jnp.float32),
        compiler_params=params(),
        cost_estimate=pl.CostEstimate(
            flops=20 * row_count * BLK,
            bytes_accessed=6 * row_count * BLK,
            transcendentals=0,
        ),
        name="place",
    )(table, *arrays)


def product(left, right):
    return jnp.dot(left, right, precision=lax.Precision.HIGHEST, preferred_element_type=jnp.float32)


def plan(
    pieces_a, pieces_b,
    sigma_sep, pattern_a, pattern_b, panel_a, panel_b, cross_b, dinv_a, dinv_b,
):
    rows_n = lax.axis_size("row")
    cols_n = lax.axis_size("col")
    row = lax.axis_index("row")
    col = lax.axis_index("col")
    local_rows, local_cols = sigma_sep.shape
    ratio = rows_n // cols_n
    row_blocks = local_rows // BLK
    col_blocks = local_cols // BLK
    width = panel_a.shape[1] * rows_n
    half_width = width // 2
    slices = width // BLK
    pair = row // 2
    diag = row // ratio
    on_diag = col == diag

    def at(r, c):
        return r * cols_n + c

    def home(r, v):
        return (v + 2 * (r // 2)) % slices

    ends = [(r, r // ratio) for r in range(rows_n)]
    spread = [
        [(at(r, d), at(r, home(r, v))) for r, d in ends if home(r, v) != d]
        for v in range(slices)
    ]
    own_v = (col + 2 * pair) % slices

    def path(d):
        if 2 * d < cols_n:
            return list(range(d)) + list(range(cols_n - 1, d - 1, -1))
        return list(range(cols_n - 1, d, -1)) + list(range(d + 1))

    def send(value, pairs):
        return lax.ppermute(value, ("row", "col"), pairs)

    core_swap = [(r, r ^ 1) for r in range(rows_n)]
    chip_swap = [(r, (r + 2) % rows_n) for r in range(rows_n)]

    core_a = lax.ppermute(panel_a, "row", core_swap)
    chip_a = lax.ppermute(panel_a, "row", chip_swap)

    lengths = (pieces_a, pieces_a, pieces_b, pieces_b)
    starts = [sum(lengths[:section]) for section in range(4)]
    count = sum(lengths)
    far = cols_n - 1
    slots = count + 2 * far
    low = jnp.where(col < diag, col, diag + cols_n - 1 - col)
    high = jnp.where(col > diag, cols_n - 1 - col, cols_n - 1 - diag + col)
    delay = 2 * jnp.where(2 * diag < cols_n, low, high)
    at_slot = jnp.arange(slots, dtype=jnp.int32) - delay
    valid = (at_slot >= 0) & (at_slot < count)
    at_slot = jnp.clip(at_slot, 0, count - 1)
    section_at = sum((at_slot >= start).astype(jnp.int32) for start in starts[1:])
    piece_at = at_slot - sum(
        jnp.where(section_at == section, start, 0) for section, start in enumerate(starts)
    )
    both = pattern_a * pattern_b
    masks = [
        lax.dynamic_slice_in_dim(pattern, index * length, length, 0)
        for index, length in ((col, col_blocks), (row, row_blocks))
        for pattern in (pattern_a, both)
    ]
    numbers = jnp.arange(row_blocks, dtype=jnp.int32)
    rank = (2 - masks[2] - masks[3]) * row_blocks + numbers
    place_of = jnp.sum((rank[None, :] < rank[:, None]).astype(jnp.int32), axis=1)
    is_at = place_of[None, :] == numbers[:, None]
    order = jnp.sum(jnp.where(is_at, numbers[None, :], 0), axis=1)
    rows_on = [jnp.sum(jnp.where(is_at, mask[None, :], 0), axis=1) for mask in masks[2:]]
    spots = piece_at[:, None] * PIECE + jnp.arange(PIECE, dtype=jnp.int32)[None, :]
    blocks = jnp.sum(
        jnp.where(spots[:, :, None] == numbers[None, None, :], order[None, None, :], 0), axis=2
    )
    table = jnp.concatenate(
        [valid.astype(jnp.int32)[:, None], section_at[:, None], blocks], axis=1
    ).reshape(-1)
    spot = slots * FIELDS
    small = jnp.stack([on_diag.astype(jnp.int32), row % 2, own_v])
    table = jnp.concatenate([table, small, *masks[:2], *rows_on, order])
    cols_a = spot + SPOTS
    cols_b = cols_a + col_blocks
    rows_a = cols_b + col_blocks
    rows_b = rows_a + row_blocks
    order_at = rows_b + row_blocks

    swapped = pair % 2 == 1

    def turn(value, axis):
        return jnp.where(swapped, jnp.roll(value, half_width, axis), value)

    cross_v = turn(turn(cross_b, 0), 1)
    cross_high = lax.reduce_precision(cross_v, 8, 7)
    cross_low = (cross_v - cross_high).astype(jnp.bfloat16)
    cross_high = cross_high.astype(jnp.bfloat16)

    def inward(slot):
        pairs = []
        for r, d in ends:
            line = path(d)
            for stop, (c, after) in enumerate(zip(line, line[1:])):
                if 0 <= slot - 2 * stop < count:
                    pairs.append((at(r, c), at(r, after)))
        return pairs

    def to_columns(value):
        total = None
        for v, pairs in enumerate(spread):
            mine = value[v * BLK : (v + 1) * BLK]
            got = jnp.where(on_diag & (own_v == v), mine, send(mine, pairs))
            total = got if total is None else total + got
        return total

    def over_cores(total):
        return total + lax.ppermute(total, "row", core_swap)

    def over_row(total):
        total = over_cores(total)
        return total + lax.ppermute(total, "row", chip_swap)

    def parts_of(length, last):
        parts = []
        first = 0
        while first < length:
            size = min(3, length - first)
            if last:
                size = 1
            parts.append((first, size))
            first += size
        return parts

    batches = [parts_of(length, section == 3) for section, length in enumerate(lengths)]
    panels = {0: join(spot, cols_a, table, panel_a, core_a, [])}
    arrived = {}
    terms = {}
    slice_parts = ([], [])
    squares = [jnp.zeros((half_width, 2 * width), jnp.float32)] * 2
    totals = [jnp.zeros((width, half_width), jnp.float32)] * 2
    waiting = {}
    message = None
    end_a = 2 * far + 2 * pieces_a - 1
    middle = pieces_a // 2

    def add_squares(half, first, length):
        squares[half] = square_sums(
            spot, order_at, table, first, length, terms[half], list(panels.values()), squares[half]
        )

    for slot in range(slots):
        if slot == 2:
            later_b = passed(panel_b, [message])
            core_b = lax.ppermute(later_b, "row", core_swap)
            chip_b = lax.ppermute(later_b, "row", chip_swap)
        if slot == starts[1] - 1:
            chip_a = passed(chip_a, [message])
            both_a = lax.ppermute(chip_a, "row", core_swap)
        if slot == starts[1]:
            panels[1] = join(spot, cols_a, table, chip_a, both_a, [message])
        if slot == starts[2] - 1:
            chip_b = passed(chip_b, [message])
            both_b = lax.ppermute(chip_b, "row", core_swap)
        if slot == starts[2]:
            panels[2] = join(spot, cols_b, table, later_b, core_b, [message])
        if slot == starts[2] + 1:
            panels[3] = join(spot, cols_b, table, chip_b, both_b, [message])
        gots = arrived.pop(slot - 2, [])
        ended = slot - 2 * far
        end = ""
        if ended >= 0:
            section = sum(ended >= start for start in starts[1:])
            piece = ended - starts[section]
            half = section % 2
            end = "ab"[section // 2]
        extra = None
        buffers = []
        places = None
        if end:
            batch = next(b for b in batches[section] if b[0] <= piece < b[0] + b[1])
            places = (piece, lengths[section], piece - batch[0], batch[1])
            if end == "a":
                buffers += terms.get(half, [None, None])
            buffers += slice_bufs if piece > batch[0] else [None, None]
        if end == "b":
            cols = slice(half * half_width, (half + 1) * half_width)
            extra = (
                terms[0] + terms[1],
                (cross_high[:, cols], cross_low[:, cols]),
                (panels[2], panels[3]),
                totals[half],
            )
        first = sum(max(0, ended) >= start for start in starts[1:])
        final = sum(slot >= start for start in starts[1:])
        after = [] if message is None else [message]
        after += waiting.pop(slot, [])
        outs = run_slot(
            slot,
            spot,
            table,
            sigma_sep,
            {section: panels[section] for section in range(first, final + 1)},
            gots,
            end,
            extra,
            after,
            buffers,
            places,
        )
        message = outs[0]
        if slot < slots - 2:
            arrived[slot] = [send(message, inward(slot))]
        if end == "a":
            terms[half] = list(outs[1:3])
        if end == "b":
            totals[half] = outs[-1]
        if end:
            start = 3 if end == "a" else 1
            slice_bufs = list(outs[start : start + 2])
            if piece == batch[0] + batch[1] - 1:
                parts = slice_parts[section // 2]
                for part in range(2):
                    got = send(slice_bufs[part], spread[2 * half + part])
                    parts.append((2 * half + part, batch[0], slice_bufs[part], got))
                    waiting.setdefault(slot + (2 if section == 3 else 7), []).append(got)
        if slot == end_a - 2:
            add_squares(0, 0, middle)
        if slot == end_a - 1:
            add_squares(0, middle, pieces_a - middle)
        if slot == end_a:
            add_squares(1, 0, pieces_a)
            whole_a = jnp.concatenate(squares, axis=0)
            whole_a = jnp.concatenate([turn(whole_a[:, :width], 1), turn(whole_a[:, width:], 1)], 1)
            sums = to_columns(whole_a)
        if slot == end_a + min(4, 2 * pieces_b - 1):
            sigma_ia = place(
                spot, rows_a, order_at, table, pieces_a, local_rows, slice_parts[0]
            )
            waiting.setdefault(slot + 1, []).append(sigma_ia)
        if slot == slots - 4:
            sums = over_cores(passed(sums, [message]))
        if slot == slots - 3:
            sums = passed(sums, [message])
            sums = sums + lax.ppermute(sums, "row", chip_swap)
            waiting.setdefault(slots - 1, []).append(sums)
    sigma_aa = dinv_a + sums[:, :width]
    image_ab = product(sigma_aa, cross_b) - sums[:, width:]
    sigma_ab = -lax.dynamic_slice_in_dim(image_ab, row * BLK, BLK, 1)
    total = to_columns(turn(jnp.concatenate(totals, axis=1), 1))
    cross_own = lax.dynamic_slice_in_dim(cross_b, col * BLK, BLK, 1)
    cross_ab = dinv_b
    for shift in range(cols_n):
        pairs = [(c, (c + shift) % cols_n) for c in range(cols_n)]
        there = lax.ppermute(image_ab, "col", pairs) if shift else image_ab
        source = (col + cols_n - shift) % cols_n
        left = lax.dynamic_slice_in_dim(cross_own, source * BLK, BLK, 0)
        cross_ab = cross_ab + product(left.T, there)
    sigma_bb = cross_ab + over_row(total)
    sigma_ib = place(spot, rows_b, order_at, table, pieces_b, local_rows, slice_parts[1])
    return (sigma_ia, sigma_aa, sigma_ib, sigma_ab, sigma_bb)


PLANS = ((3, 3),)


def per_device(sigma_sep, pattern_a, pattern_b, panel_a, panel_b, cross_b, dinv_a, dinv_b):
    bands = lax.axis_size("row")
    most_a = jnp.max(jnp.sum(pattern_a.reshape(bands, -1), axis=1))
    most_b = jnp.max(jnp.sum((pattern_a * pattern_b).reshape(bands, -1), axis=1))
    fits = [(most_a <= a * PIECE) & (most_b <= b * PIECE) for a, b in PLANS]
    which = jnp.argmax(jnp.stack(fits))
    return lax.switch(
        which,
        [functools.partial(plan, a, b) for a, b in PLANS],
        sigma_sep,
        pattern_a,
        pattern_b,
        panel_a,
        panel_b,
        cross_b,
        dinv_a,
        dinv_b,
    )


def broadcast(value, axis, root):
    mine = lax.axis_index(axis) == root
    return lax.psum(jnp.where(mine, value, jnp.zeros_like(value)), axis)


def block_mask(pattern, first_row, row_count):
    blocks = (first_row + jnp.arange(row_count, dtype=jnp.int32)) // BLK
    block_ids = jnp.arange(pattern.shape[0], dtype=jnp.int32)
    matches = (blocks[:, None] == block_ids[None, :]).astype(jnp.float32)
    return product(matches, pattern.astype(jnp.float32)[:, None])


def per_device_any(sigma_sep, pattern_a, pattern_b, panel_a, panel_b, cross_b, dinv_a, dinv_b):
    row_devices = lax.axis_size("row")
    col_devices = lax.axis_size("col")
    row_index = lax.axis_index("row")
    col_index = lax.axis_index("col")
    local_rows = sigma_sep.shape[0]
    local_cols = sigma_sep.shape[1]
    panel_width = panel_a.shape[1] * row_devices
    slice_width = panel_width // col_devices
    band_width = panel_width // row_devices
    row_ratio = row_devices // col_devices
    pattern_both = pattern_a * pattern_b
    masked_a = (
        panel_a.astype(jnp.float32) * block_mask(pattern_a, col_index * local_cols, local_cols)
    ).astype(jnp.bfloat16)
    masked_b = (
        panel_b.astype(jnp.float32) * block_mask(pattern_both, col_index * local_cols, local_cols)
    ).astype(jnp.bfloat16)
    mask_a_rows = block_mask(pattern_a, row_index * local_rows, local_rows)
    mask_b_rows = block_mask(pattern_both, row_index * local_rows, local_rows)
    source_col = row_index // row_ratio
    offset = row_index % row_ratio * local_rows

    def own_rows(gathered):
        return lax.dynamic_slice_in_dim(gathered, offset, local_rows, 0)

    full_a = lax.all_gather(masked_a, "row", axis=1, tiled=True)
    rows_a = broadcast(own_rows(full_a), "col", source_col)
    rows_a32 = rows_a.astype(jnp.float32)
    partial_a = jnp.dot(sigma_sep, full_a, preferred_element_type=jnp.float32)
    image_a = lax.psum_scatter(partial_a, "col", scatter_dimension=1, tiled=True)
    sigma_ia = -mask_a_rows * image_a
    quadratic_a = lax.psum(product(image_a.T, rows_a32), "row")
    sigma_aa = dinv_a + quadratic_a
    full_b = lax.all_gather(masked_b, "row", axis=1, tiled=True)
    rows_b = broadcast(own_rows(full_b), "col", source_col)
    rows_b32 = rows_b.astype(jnp.float32)
    cross_rows = lax.dynamic_slice_in_dim(cross_b, col_index * slice_width, slice_width, 0)
    cross_cols = lax.dynamic_slice_in_dim(cross_b, row_index * band_width, band_width, 1)
    partial_b = jnp.dot(sigma_sep, full_b, preferred_element_type=jnp.float32) + product(
        sigma_ia, cross_rows
    )
    image_b = lax.psum_scatter(partial_b, "col", scatter_dimension=1, tiled=True)
    sigma_ib = -mask_b_rows * image_b
    upper_part = lax.psum_scatter(
        product(sigma_ia.T, rows_b32), "row", scatter_dimension=1, tiled=True
    )
    image_ab = upper_part + product(sigma_aa, cross_cols)
    sigma_ab = -image_ab
    first_term = product(rows_b32.T, image_b)
    second_term = product(cross_rows.T, image_ab)
    blank = jnp.zeros((panel_width, panel_width), jnp.float32)
    placed = lax.dynamic_update_slice_in_dim(blank, first_term, col_index * slice_width, 1)
    placed = placed + lax.dynamic_update_slice_in_dim(blank, second_term, row_index * band_width, 1)
    share_b = lax.psum_scatter(placed, "col", scatter_dimension=0, tiled=True)
    total_bb = lax.psum(share_b, "row")
    sigma_bb = dinv_b + total_bb
    return (sigma_ia, sigma_aa, sigma_ib, sigma_ab, sigma_bb)


def tuned(mesh, sigma_sep, panel_a):
    rows_n, cols_n = mesh.shape["row"], mesh.shape["col"]
    rows = sigma_sep.shape[0] // (mesh.shape["groups"] * rows_n)
    cols = sigma_sep.shape[1] // cols_n
    return (
        rows_n == 4
        and cols_n == 4
        and panel_a.shape[1] == 4 * BLK
        and rows == BLK * PIECE * PLANS[-1][0]
        and cols % (DEPTH_STEPS * BLK) == 0
    )


def solution(mesh):
    placed = (
        P(("groups", "row"), "col"),
        P(),
        P(),
        P(("groups", "col"), "row"),
        P(("groups", "col"), "row"),
        P("groups", None),
        P(("groups", "col"), None),
        P(("groups", "col"), None),
    )
    out_placed = (
        P(("groups", "row"), "col"),
        P(("groups", "col"), None),
        P(("groups", "row"), "col"),
        P(("groups", "col"), "row"),
        P(("groups", "col"), None),
    )

    def run(sigma_sep, pattern_a, pattern_b, panel_a, panel_b, cross_b, dinv_a, dinv_b):
        body = per_device if tuned(mesh, sigma_sep, panel_a) else per_device_any
        return jax.shard_map(
            body, mesh=mesh, in_specs=placed, out_specs=out_placed, check_vma=False
        )(sigma_sep, pattern_a, pattern_b, panel_a, panel_b, cross_b, dinv_a, dinv_b)

    return run
```

```python
import functools

import jax
import jax.numpy as jnp
from jax import lax
from jax.experimental import pallas as pl
from jax.experimental.pallas import tpu as pltpu
from jax.sharding import PartitionSpec as P

BLK = 128
TOP = 32704.0
STEPS = 64.0
LN2 = 0.6931471805599453
ROUND = 1.5 * 2.0**23
TAIL = 16
VMEM = 40 * 2**20
SLOT_VMEM = 50 * 2**20

PIECE = 10
DEPTH_STEPS = 3


def code_of(values):
    top = jnp.max(jnp.abs(values), axis=0, keepdims=True)
    return jnp.ceil(jnp.log(jnp.maximum(top, 1e-30)) * (STEPS / LN2))


def scale_of(code):
    return jnp.exp(code * (LN2 / STEPS))


def coded(values, code):
    values = (values * (TOP / scale_of(code)) + ROUND) - ROUND
    return values.astype(jnp.int32).astype(jnp.int16)


def pick(table, row):
    rows = lax.broadcasted_iota(jnp.int32, table.shape, 0)
    return jnp.sum(jnp.where(rows == row, table, 0.0), axis=0, keepdims=True)


def put(table_ref, row, value):
    rows = lax.broadcasted_iota(jnp.int32, table_ref.shape, 0)
    table_ref[...] = jnp.where(rows == row, value, table_ref[...])


def decoded(message, block):
    table = message[PIECE * BLK :, :].astype(jnp.int32).astype(jnp.float32)
    values = message[block * BLK : (block + 1) * BLK, :].astype(jnp.int32).astype(jnp.float32)
    return values * (scale_of(pick(table, block)) * (1.0 / TOP))


def encode(block, values, codes, outs):
    code = code_of(values)
    values = coded(values, code)
    columns = values.shape[1] // len(outs)
    for part, out in enumerate(outs):
        out[block * BLK : (block + 1) * BLK, :] = values[:, part * columns : (part + 1) * columns]
    rows = lax.broadcasted_iota(jnp.int32, codes.shape, 0)
    return jnp.where(rows == block, code, codes)


def close(codes, outs):
    codes = codes.astype(jnp.int32).astype(jnp.int16)
    columns = codes.shape[1] // len(outs)
    for part, out in enumerate(outs):
        out[PIECE * BLK :, :] = codes[:, part * columns : (part + 1) * columns]


def split(values):
    high = values.astype(jnp.bfloat16)
    return high, (values - high.astype(jnp.float32)).astype(jnp.bfloat16)


def over_rows(left, right):
    return lax.dot_general(
        left, right, (((0,), (0,)), ((), ())), preferred_element_type=jnp.float32
    )


def dot(left, right):
    return jnp.dot(left, right, preferred_element_type=jnp.float32)


def whole(shape):
    return pl.BlockSpec(shape, lambda i, *_: (0,) * len(shape))


def params(limit=VMEM):
    return pltpu.CompilerParams(vmem_limit_bytes=limit)


FIELDS = 2 + PIECE
ENDS, PARITY, OWN = range(3)
SPOTS = 3


def here():
    return pl.BlockSpec(memory_space=pl.ANY)


def far_off():
    return pl.BlockSpec(memory_space=pltpu.HBM)


def join_kernel(spot, mask, blocks, table, mine_ref, theirs_ref, *refs):
    out_ref = refs[-1]
    even = table[spot + PARITY] == 0
    for block in range(blocks):
        rows = slice(block * BLK, (block + 1) * BLK)
        mine, theirs = mine_ref[rows, :], theirs_ref[rows, :]
        on = table[mask + pl.program_id(0) * blocks + block] == 1
        zero = jnp.zeros_like(mine)
        out_ref[rows, :BLK] = jnp.where(on, jnp.where(even, mine, theirs), zero)
        out_ref[rows, BLK:] = jnp.where(on, jnp.where(even, theirs, mine), zero)


def join(spot, mask, table, mine, theirs, after):
    rows = mine.shape[0]
    blocks = rows // (BLK * DEPTH_STEPS)
    block = pl.BlockSpec((blocks * BLK, BLK), lambda i, *_: (i, 0))
    return pl.pallas_call(
        functools.partial(join_kernel, spot, mask, blocks),
        grid_spec=pltpu.PrefetchScalarGridSpec(
            num_scalar_prefetch=1,
            grid=(DEPTH_STEPS,),
            in_specs=[block, block] + [here()] * len(after),
            out_specs=pl.BlockSpec((blocks * BLK, 2 * BLK), lambda i, *_: (i, 0)),
        ),
        out_shape=pltpu.HBM((rows, 2 * BLK), mine.dtype),
        compiler_params=params(),
        cost_estimate=pl.CostEstimate(
            flops=rows * BLK, bytes_accessed=8 * rows * BLK, transcendentals=0
        ),
        name="join",
    )(table, mine, theirs, *after)


def pass_kernel(in_ref, *refs):
    refs[-1][...] = in_ref[...]


def passed(value, after):
    block = pl.BlockSpec(value.shape, lambda i: (0,) * value.ndim)
    return pl.pallas_call(
        pass_kernel,
        grid=(1,),
        in_specs=[block] + [here()] * len(after),
        out_specs=block,
        out_shape=jax.ShapeDtypeStruct(value.shape, value.dtype),
        compiler_params=params(),
        cost_estimate=pl.CostEstimate(
            flops=value.size, bytes_accessed=4 * value.size, transcendentals=0
        ),
        name="passed",
    )(value, *after)


def slot_kernel(slot, spot, sections, gots, end, waits, aliases, table, *refs):
    refs = list(refs)

    def take(count):
        taken = refs[:count]
        del refs[:count]
        return taken

    (sigma,) = take(1)
    panels = take(len(sections))
    got_refs = take(gots)
    if end == "b":
        terms = take(4)
        cross_high, cross_low = take(2)
        rows_0, rows_1 = take(PIECE), take(PIECE)
        (total_in,) = take(1)
    take(waits + aliases)
    (msg_ref,) = take(1)
    if end == "a":
        high_ref, low_ref = take(2)
    if end:
        slice_refs = [ref.at[0] for ref in take(2)]
    if end == "b":
        (total_ref,) = take(1)
    acc, left, rhs, sems = take(4)
    valid = table[slot * FIELDS] == 1
    ends = table[spot + ENDS] == 1
    part = rhs.shape[0] // DEPTH_STEPS

    def panel_copy(panel, which):
        span = pl.ds(which * part, part)
        return pltpu.make_async_copy(panel.at[span, :], rhs.at[span, :], sems.at[which, PIECE])

    def sigma_copy(block, which):
        first = pl.multiple_of(table[slot * FIELDS + 2 + block] * BLK, BLK)
        span = pl.ds(which * part, part)
        return pltpu.make_async_copy(
            sigma.at[pl.ds(first, BLK), span],
            left.at[pl.ds(block * BLK, BLK), span],
            sems.at[which, block],
        )

    @pl.when(valid)
    def _():
        for which in range(DEPTH_STEPS):
            for section, panel in zip(sections, panels):

                @pl.when(table[slot * FIELDS + 1] == section)
                def _():
                    panel_copy(panel, which).start()

            for block in range(PIECE):
                sigma_copy(block, which).start()
        for which in range(DEPTH_STEPS):
            panel_copy(panels[0], which).wait()
            for block in range(PIECE):
                sigma_copy(block, which).wait()
            span = slice(which * part, (which + 1) * part)
            values = dot(left[:, span], rhs[span, :])
            if which:
                acc[...] += values
            else:
                acc[...] = values

    def values_of(block):
        values = acc[block * BLK : (block + 1) * BLK, :]
        for got_ref in got_refs:
            values = values + decoded(got_ref, block)
        return values

    blank = jnp.zeros((TAIL, acc.shape[1]), jnp.float32)

    @pl.when(valid & jnp.logical_not(ends))
    def _():
        codes = blank
        for block in range(PIECE):
            codes = encode(block, values_of(block), codes, [msg_ref])
        close(codes, [msg_ref])

    if end == "a":

        @pl.when(ends & jnp.logical_not(valid))
        def _():
            high_ref[...] = jnp.zeros_like(high_ref)
            low_ref[...] = jnp.zeros_like(low_ref)

        @pl.when(ends & valid)
        def _():
            codes = blank
            for block in range(PIECE):
                values = values_of(block)
                rows = slice(block * BLK, (block + 1) * BLK)
                high_ref[rows, :], low_ref[rows, :] = split(values)
                codes = encode(block, values, codes, slice_refs)
            close(codes, slice_refs)

    if end == "b":

        @pl.when(ends & jnp.logical_not(valid))
        def _():
            total_ref[...] = total_in[...]

        @pl.when(ends & valid)
        def _():
            high = jnp.concatenate([terms[0][...], terms[2][...]], axis=1)
            low = jnp.concatenate([terms[1][...], terms[3][...]], axis=1)
            acc[...] -= (
                dot(high, cross_high[...])
                + dot(high, cross_low[...])
                + dot(low, cross_high[...])
            )
            codes = blank
            for block in range(PIECE):
                values = values_of(block)
                acc[block * BLK : (block + 1) * BLK, :] = values
                codes = encode(block, values, codes, slice_refs)
            close(codes, slice_refs)
            high, low = split(acc[...])
            rows = jnp.concatenate(
                [jnp.concatenate([x[...], y[...]], axis=1) for x, y in zip(rows_0, rows_1)],
                axis=0,
            )
            total_ref[...] = total_in[...] + (over_rows(rows, high) + over_rows(rows, low))


def run_slot(slot, spot, table, sigma, panels, gots, end, extra, after, buffers, spots):
    depth = sigma.shape[1]
    width = next(iter(panels.values())).shape[1]
    rows = PIECE * BLK
    base = slot * FIELDS

    def panel_row(which):
        return lambda i, table: (table[base + 2 + which], 0)

    in_specs = [far_off()] * (1 + len(panels))
    operands = [sigma] + list(panels.values())
    message = (rows + TAIL, width)
    in_specs += [whole(message)] * len(gots)
    operands += gots
    out_specs = [whole(message)]
    out_shape = [jax.ShapeDtypeStruct(message, jnp.int16)]
    if end:
        piece, pieces, place_in, places = spots
    if end == "a":
        out_specs += [pl.BlockSpec((rows, width), lambda i, *_: (piece, 0))] * 2
        out_shape += [pltpu.HBM((pieces * rows, width), jnp.bfloat16)] * 2
    if end:
        slice_message = (1, rows + TAIL, width // 2)
        out_specs += [pl.BlockSpec(slice_message, lambda i, *_: (place_in, 0, 0))] * 2
        out_shape += [pltpu.HBM((places,) + slice_message[1:], jnp.int16)] * 2
    if end == "b":
        terms, cross, both, total = extra
        in_specs += [pl.BlockSpec((rows, width), lambda i, *_: (piece, 0))] * 4
        in_specs += [whole((2 * width, width))] * 2
        for _ in range(2):
            in_specs += [pl.BlockSpec((BLK, width), panel_row(which)) for which in range(PIECE)]
        in_specs.append(whole((2 * width, width)))
        operands += [*terms, *cross] + [both[0]] * PIECE + [both[1]] * PIECE + [total]
        out_specs.append(whole((2 * width, width)))
        out_shape.append(jax.ShapeDtypeStruct((2 * width, width), jnp.float32))
    in_specs += [here()] * len(after)
    operands += after
    aliases = {}
    count = 0
    for which, buffer in enumerate(buffers):
        if buffer is not None:
            aliases[1 + len(operands)] = 1 + which
            in_specs.append(far_off())
            operands.append(buffer)
            count += 1
    return pl.pallas_call(
        functools.partial(
            slot_kernel, slot, spot, tuple(panels), len(gots), end, len(after), count
        ),
        grid_spec=pltpu.PrefetchScalarGridSpec(
            num_scalar_prefetch=1,
            grid=(1,),
            in_specs=in_specs,
            out_specs=out_specs,
            scratch_shapes=[
                pltpu.VMEM((rows, width), jnp.float32),
                pltpu.VMEM((rows, depth), jnp.bfloat16),
                pltpu.VMEM((depth, width), jnp.bfloat16),
                pltpu.SemaphoreType.DMA((DEPTH_STEPS, PIECE + 1)),
            ],
        ),
        out_shape=out_shape,
        input_output_aliases=aliases,
        compiler_params=params(SLOT_VMEM),
        cost_estimate=pl.CostEstimate(
            flops=rows * width,
            bytes_accessed=rows * width,
            transcendentals=0,
        ),
        name="slot",
    )(table, *operands)


def square_kernel(spot, table, *refs):
    high_ref, low_ref, *panels, in_ref, out_ref = refs

    @pl.when(table[spot + ENDS] == 1)
    def _():
        @pl.when(pl.program_id(0) == 0)
        def _():
            out_ref[...] = in_ref[...]

        rows = jnp.concatenate(
            [
                jnp.concatenate([ref[...] for ref in panels[first : first + PIECE]], axis=0)
                for first in range(0, len(panels), PIECE)
            ],
            axis=1,
        )
        out_ref[...] += over_rows(high_ref[...], rows) + over_rows(low_ref[...], rows)


def square_sums(spot, order, table, first, count, terms, panels, total):
    width = terms[0].shape[1]
    rows = PIECE * BLK
    term = pl.BlockSpec((rows, width), lambda i, *_: (first + i, 0))

    def panel_row(which):
        return lambda i, table: (table[order + (first + i) * PIECE + which], 0)

    shape = (width, len(panels) * width)
    blocks = [pl.BlockSpec((BLK, width), panel_row(which)) for which in range(PIECE)]
    return pl.pallas_call(
        functools.partial(square_kernel, spot),
        grid_spec=pltpu.PrefetchScalarGridSpec(
            num_scalar_prefetch=1,
            grid=(count,),
            in_specs=[term] * 2 + blocks * len(panels) + [whole(shape)],
            out_specs=whole(shape),
        ),
        out_shape=jax.ShapeDtypeStruct(shape, jnp.float32),
        compiler_params=params(),
        cost_estimate=pl.CostEstimate(
            flops=16 * count * rows * width * width,
            bytes_accessed=12 * count * rows * width + 32 * width * width,
            transcendentals=0,
        ),
        name="square_sums",
    )(table, *terms, *[panel for panel in panels for _ in range(PIECE)], total)


def place_kernel(spot, on, order, pieces, parts, table, *refs):
    arrays = refs[: 2 * len(parts)]
    out_ref, held, sem = refs[2 * len(parts) :]
    own = table[spot + OWN]
    ends = table[spot + ENDS] == 1
    for which, (v, start, count) in enumerate(parts):
        for side, wanted in ((0, ends), (1, jnp.logical_not(ends))):

            @pl.when((own == v) & wanted)
            def _():
                source = arrays[2 * which + side]
                copy = pltpu.make_async_copy(source, held.at[pl.ds(start, count)], sem)
                copy.start()
                copy.wait()

    out_ref[...] = jnp.zeros_like(out_ref)

    @pl.loop(0, pieces)
    def _(piece):
        message = held.at[piece]
        for block in range(PIECE):
            which = piece * PIECE + block
            first = pl.multiple_of(table[order + which] * BLK, BLK)
            values = jnp.where(table[on + which] == 1, -decoded(message, block), 0.0)
            out_ref[pl.ds(first, BLK), :] = values


def place(spot, on, order, table, pieces, row_count, parts):
    message = parts[0][2].shape[1:]
    ranges = tuple((v, start, mine.shape[0]) for v, start, mine, _ in parts)
    arrays = [array for part in parts for array in part[2:]]
    return pl.pallas_call(
        functools.partial(place_kernel, spot, on, order, pieces, ranges),
        grid_spec=pltpu.PrefetchScalarGridSpec(
            num_scalar_prefetch=1,
            grid=(1,),
            in_specs=[far_off()] * len(arrays),
            out_specs=whole((row_count, BLK)),
            scratch_shapes=[
                pltpu.VMEM((pieces,) + message, jnp.int16),
                pltpu.SemaphoreType.DMA(()),
            ],
        ),
        out_shape=jax.ShapeDtypeStruct((row_count, BLK), jnp.float32),
        compiler_params=params(),
        cost_estimate=pl.CostEstimate(
            flops=20 * row_count * BLK,
            bytes_accessed=6 * row_count * BLK,
            transcendentals=0,
        ),
        name="place",
    )(table, *arrays)


def product(left, right):
    return jnp.dot(left, right, precision=lax.Precision.HIGHEST, preferred_element_type=jnp.float32)


def plan(
    pieces_a, pieces_b,
    sigma_sep, pattern_a, pattern_b, panel_a, panel_b, cross_b, dinv_a, dinv_b,
):
    rows_n = lax.axis_size("row")
    cols_n = lax.axis_size("col")
    row = lax.axis_index("row")
    col = lax.axis_index("col")
    local_rows, local_cols = sigma_sep.shape
    ratio = rows_n // cols_n
    row_blocks = local_rows // BLK
    col_blocks = local_cols // BLK
    width = panel_a.shape[1] * rows_n
    half_width = width // 2
    slices = width // BLK
    pair = row // 2
    diag = row // ratio
    on_diag = col == diag

    def at(r, c):
        return r * cols_n + c

    def home(r, v):
        return (v + 2 * (r // 2)) % slices

    ends = [(r, r // ratio) for r in range(rows_n)]
    spread = [
        [(at(r, d), at(r, home(r, v))) for r, d in ends if home(r, v) != d]
        for v in range(slices)
    ]
    own_v = (col + 2 * pair) % slices

    def path(d):
        if 2 * d < cols_n:
            return list(range(d)) + list(range(cols_n - 1, d - 1, -1))
        return list(range(cols_n - 1, d, -1)) + list(range(d + 1))

    def send(value, pairs):
        return lax.ppermute(value, ("row", "col"), pairs)

    core_swap = [(r, r ^ 1) for r in range(rows_n)]
    chip_swap = [(r, (r + 2) % rows_n) for r in range(rows_n)]

    core_a = lax.ppermute(panel_a, "row", core_swap)
    chip_a = lax.ppermute(panel_a, "row", chip_swap)

    lengths = (pieces_a, pieces_a, pieces_b, pieces_b)
    starts = [sum(lengths[:section]) for section in range(4)]
    count = sum(lengths)
    far = cols_n - 1
    slots = count + 2 * far
    low = jnp.where(col < diag, col, diag + cols_n - 1 - col)
    high = jnp.where(col > diag, cols_n - 1 - col, cols_n - 1 - diag + col)
    delay = 2 * jnp.where(2 * diag < cols_n, low, high)
    at_slot = jnp.arange(slots, dtype=jnp.int32) - delay
    valid = (at_slot >= 0) & (at_slot < count)
    at_slot = jnp.clip(at_slot, 0, count - 1)
    section_at = sum((at_slot >= start).astype(jnp.int32) for start in starts[1:])
    piece_at = at_slot - sum(
        jnp.where(section_at == section, start, 0) for section, start in enumerate(starts)
    )
    both = pattern_a * pattern_b
    masks = [
        lax.dynamic_slice_in_dim(pattern, index * length, length, 0)
        for index, length in ((col, col_blocks), (row, row_blocks))
        for pattern in (pattern_a, both)
    ]
    numbers = jnp.arange(row_blocks, dtype=jnp.int32)
    rank = (2 - masks[2] - masks[3]) * row_blocks + numbers
    place_of = jnp.sum((rank[None, :] < rank[:, None]).astype(jnp.int32), axis=1)
    is_at = place_of[None, :] == numbers[:, None]
    order = jnp.sum(jnp.where(is_at, numbers[None, :], 0), axis=1)
    rows_on = [jnp.sum(jnp.where(is_at, mask[None, :], 0), axis=1) for mask in masks[2:]]
    spots = piece_at[:, None] * PIECE + jnp.arange(PIECE, dtype=jnp.int32)[None, :]
    blocks = jnp.sum(
        jnp.where(spots[:, :, None] == numbers[None, None, :], order[None, None, :], 0), axis=2
    )
    left_a, left_b = (jnp.sum(mask) for mask in rows_on)
    valid &= piece_at * PIECE < jnp.where(section_at < 2, left_a, left_b)
    table = jnp.concatenate(
        [valid.astype(jnp.int32)[:, None], section_at[:, None], blocks], axis=1
    ).reshape(-1)
    spot = slots * FIELDS
    small = jnp.stack([on_diag.astype(jnp.int32), row % 2, own_v])
    table = jnp.concatenate([table, small, *masks[:2], *rows_on, order])
    cols_a = spot + SPOTS
    cols_b = cols_a + col_blocks
    rows_a = cols_b + col_blocks
    rows_b = rows_a + row_blocks
    order_at = rows_b + row_blocks

    swapped = pair % 2 == 1

    def turn(value, axis):
        return jnp.where(swapped, jnp.roll(value, half_width, axis), value)

    cross_v = turn(turn(cross_b, 0), 1)
    cross_high = lax.reduce_precision(cross_v, 8, 7)
    cross_low = (cross_v - cross_high).astype(jnp.bfloat16)
    cross_high = cross_high.astype(jnp.bfloat16)

    def inward(slot):
        pairs = []
        for r, d in ends:
            line = path(d)
            for stop, (c, after) in enumerate(zip(line, line[1:])):
                if 0 <= slot - 2 * stop < count:
                    pairs.append((at(r, c), at(r, after)))
        return pairs

    def to_columns(value):
        total = None
        for v, pairs in enumerate(spread):
            mine = value[v * BLK : (v + 1) * BLK]
            got = jnp.where(on_diag & (own_v == v), mine, send(mine, pairs))
            total = got if total is None else total + got
        return total

    def over_cores(total):
        return total + lax.ppermute(total, "row", core_swap)

    def over_row(total):
        total = over_cores(total)
        return total + lax.ppermute(total, "row", chip_swap)

    def parts_of(length, last):
        parts = []
        first = 0
        while first < length:
            size = min(3, length - first)
            if last:
                size = 1
            parts.append((first, size))
            first += size
        return parts

    batches = [parts_of(length, section == 3) for section, length in enumerate(lengths)]
    panels = {0: join(spot, cols_a, table, panel_a, core_a, [])}
    arrived = {}
    terms = {}
    slice_parts = ([], [])
    squares = [jnp.zeros((half_width, 2 * width), jnp.float32)] * 2
    totals = [jnp.zeros((width, half_width), jnp.float32)] * 2
    waiting = {}
    message = None
    end_a = 2 * far + 2 * pieces_a - 1
    middle = pieces_a // 2

    def add_squares(half, first, length):
        squares[half] = square_sums(
            spot, order_at, table, first, length, terms[half], list(panels.values()), squares[half]
        )

    for slot in range(slots):
        if slot == 2:
            later_b = passed(panel_b, [message])
            core_b = lax.ppermute(later_b, "row", core_swap)
            chip_b = lax.ppermute(later_b, "row", chip_swap)
        if slot == starts[1] - 1:
            chip_a = passed(chip_a, [message])
            both_a = lax.ppermute(chip_a, "row", core_swap)
        if slot == starts[1]:
            panels[1] = join(spot, cols_a, table, chip_a, both_a, [message])
        if slot == starts[2] - 1:
            chip_b = passed(chip_b, [message])
            both_b = lax.ppermute(chip_b, "row", core_swap)
        if slot == starts[2]:
            panels[2] = join(spot, cols_b, table, later_b, core_b, [message])
        if slot == starts[2] + 1:
            panels[3] = join(spot, cols_b, table, chip_b, both_b, [message])
        gots = arrived.pop(slot - 2, [])
        ended = slot - 2 * far
        end = ""
        if ended >= 0:
            section = sum(ended >= start for start in starts[1:])
            piece = ended - starts[section]
            half = section % 2
            end = "ab"[section // 2]
        extra = None
        buffers = []
        places = None
        if end:
            batch = next(b for b in batches[section] if b[0] <= piece < b[0] + b[1])
            places = (piece, lengths[section], piece - batch[0], batch[1])
            if end == "a":
                buffers += terms.get(half, [None, None])
            buffers += slice_bufs if piece > batch[0] else [None, None]
        if end == "b":
            cols = slice(half * half_width, (half + 1) * half_width)
            extra = (
                terms[0] + terms[1],
                (cross_high[:, cols], cross_low[:, cols]),
                (panels[2], panels[3]),
                totals[half],
            )
        first = sum(max(0, ended) >= start for start in starts[1:])
        final = sum(slot >= start for start in starts[1:])
        after = [] if message is None else [message]
        after += waiting.pop(slot, [])
        outs = run_slot(
            slot,
            spot,
            table,
            sigma_sep,
            {section: panels[section] for section in range(first, final + 1)},
            gots,
            end,
            extra,
            after,
            buffers,
            places,
        )
        message = outs[0]
        if slot < slots - 2:
            arrived[slot] = [send(message, inward(slot))]
        if end == "a":
            terms[half] = list(outs[1:3])
        if end == "b":
            totals[half] = outs[-1]
        if end:
            start = 3 if end == "a" else 1
            slice_bufs = list(outs[start : start + 2])
            if piece == batch[0] + batch[1] - 1:
                parts = slice_parts[section // 2]
                for part in range(2):
                    got = send(slice_bufs[part], spread[2 * half + part])
                    parts.append((2 * half + part, batch[0], slice_bufs[part], got))
                    waiting.setdefault(slot + (2 if section == 3 else 7), []).append(got)
        if slot == end_a - 2:
            add_squares(0, 0, middle)
        if slot == end_a - 1:
            add_squares(0, middle, pieces_a - middle)
        if slot == end_a:
            add_squares(1, 0, pieces_a)
            whole_a = jnp.concatenate(squares, axis=0)
            whole_a = jnp.concatenate([turn(whole_a[:, :width], 1), turn(whole_a[:, width:], 1)], 1)
            sums = to_columns(whole_a)
        if slot == end_a + min(4, 2 * pieces_b - 1):
            sigma_ia = place(
                spot, rows_a, order_at, table, pieces_a, local_rows, slice_parts[0]
            )
            waiting.setdefault(slot + 1, []).append(sigma_ia)
        if slot == slots - 4:
            sums = over_cores(passed(sums, [message]))
        if slot == slots - 3:
            sums = passed(sums, [message])
            sums = sums + lax.ppermute(sums, "row", chip_swap)
            waiting.setdefault(slots - 1, []).append(sums)
    sigma_aa = dinv_a + sums[:, :width]
    image_ab = product(sigma_aa, cross_b) - sums[:, width:]
    sigma_ab = -lax.dynamic_slice_in_dim(image_ab, row * BLK, BLK, 1)
    total = to_columns(turn(jnp.concatenate(totals, axis=1), 1))
    cross_own = lax.dynamic_slice_in_dim(cross_b, col * BLK, BLK, 1)
    cross_ab = dinv_b
    for shift in range(cols_n):
        pairs = [(c, (c + shift) % cols_n) for c in range(cols_n)]
        there = lax.ppermute(image_ab, "col", pairs) if shift else image_ab
        source = (col + cols_n - shift) % cols_n
        left = lax.dynamic_slice_in_dim(cross_own, source * BLK, BLK, 0)
        cross_ab = cross_ab + product(left.T, there)
    sigma_bb = cross_ab + over_row(total)
    sigma_ib = place(spot, rows_b, order_at, table, pieces_b, local_rows, slice_parts[1])
    return (sigma_ia, sigma_aa, sigma_ib, sigma_ab, sigma_bb)


PLANS = ((3, 3),)


def per_device(sigma_sep, pattern_a, pattern_b, panel_a, panel_b, cross_b, dinv_a, dinv_b):
    bands = lax.axis_size("row")
    most_a = jnp.max(jnp.sum(pattern_a.reshape(bands, -1), axis=1))
    most_b = jnp.max(jnp.sum((pattern_a * pattern_b).reshape(bands, -1), axis=1))
    fits = [(most_a <= a * PIECE) & (most_b <= b * PIECE) for a, b in PLANS]
    which = jnp.argmax(jnp.stack(fits))
    return lax.switch(
        which,
        [functools.partial(plan, a, b) for a, b in PLANS],
        sigma_sep,
        pattern_a,
        pattern_b,
        panel_a,
        panel_b,
        cross_b,
        dinv_a,
        dinv_b,
    )


def broadcast(value, axis, root):
    mine = lax.axis_index(axis) == root
    return lax.psum(jnp.where(mine, value, jnp.zeros_like(value)), axis)


def block_mask(pattern, first_row, row_count):
    blocks = (first_row + jnp.arange(row_count, dtype=jnp.int32)) // BLK
    block_ids = jnp.arange(pattern.shape[0], dtype=jnp.int32)
    matches = (blocks[:, None] == block_ids[None, :]).astype(jnp.float32)
    return product(matches, pattern.astype(jnp.float32)[:, None])


def per_device_any(sigma_sep, pattern_a, pattern_b, panel_a, panel_b, cross_b, dinv_a, dinv_b):
    row_devices = lax.axis_size("row")
    col_devices = lax.axis_size("col")
    row_index = lax.axis_index("row")
    col_index = lax.axis_index("col")
    local_rows = sigma_sep.shape[0]
    local_cols = sigma_sep.shape[1]
    panel_width = panel_a.shape[1] * row_devices
    slice_width = panel_width // col_devices
    band_width = panel_width // row_devices
    row_ratio = row_devices // col_devices
    pattern_both = pattern_a * pattern_b
    masked_a = (
        panel_a.astype(jnp.float32) * block_mask(pattern_a, col_index * local_cols, local_cols)
    ).astype(jnp.bfloat16)
    masked_b = (
        panel_b.astype(jnp.float32) * block_mask(pattern_both, col_index * local_cols, local_cols)
    ).astype(jnp.bfloat16)
    mask_a_rows = block_mask(pattern_a, row_index * local_rows, local_rows)
    mask_b_rows = block_mask(pattern_both, row_index * local_rows, local_rows)
    source_col = row_index // row_ratio
    offset = row_index % row_ratio * local_rows

    def own_rows(gathered):
        return lax.dynamic_slice_in_dim(gathered, offset, local_rows, 0)

    full_a = lax.all_gather(masked_a, "row", axis=1, tiled=True)
    rows_a = broadcast(own_rows(full_a), "col", source_col)
    rows_a32 = rows_a.astype(jnp.float32)
    partial_a = jnp.dot(sigma_sep, full_a, preferred_element_type=jnp.float32)
    image_a = lax.psum_scatter(partial_a, "col", scatter_dimension=1, tiled=True)
    sigma_ia = -mask_a_rows * image_a
    quadratic_a = lax.psum(product(image_a.T, rows_a32), "row")
    sigma_aa = dinv_a + quadratic_a
    full_b = lax.all_gather(masked_b, "row", axis=1, tiled=True)
    rows_b = broadcast(own_rows(full_b), "col", source_col)
    rows_b32 = rows_b.astype(jnp.float32)
    cross_rows = lax.dynamic_slice_in_dim(cross_b, col_index * slice_width, slice_width, 0)
    cross_cols = lax.dynamic_slice_in_dim(cross_b, row_index * band_width, band_width, 1)
    partial_b = jnp.dot(sigma_sep, full_b, preferred_element_type=jnp.float32) + product(
        sigma_ia, cross_rows
    )
    image_b = lax.psum_scatter(partial_b, "col", scatter_dimension=1, tiled=True)
    sigma_ib = -mask_b_rows * image_b
    upper_part = lax.psum_scatter(
        product(sigma_ia.T, rows_b32), "row", scatter_dimension=1, tiled=True
    )
    image_ab = upper_part + product(sigma_aa, cross_cols)
    sigma_ab = -image_ab
    first_term = product(rows_b32.T, image_b)
    second_term = product(cross_rows.T, image_ab)
    blank = jnp.zeros((panel_width, panel_width), jnp.float32)
    placed = lax.dynamic_update_slice_in_dim(blank, first_term, col_index * slice_width, 1)
    placed = placed + lax.dynamic_update_slice_in_dim(blank, second_term, row_index * band_width, 1)
    share_b = lax.psum_scatter(placed, "col", scatter_dimension=0, tiled=True)
    total_bb = lax.psum(share_b, "row")
    sigma_bb = dinv_b + total_bb
    return (sigma_ia, sigma_aa, sigma_ib, sigma_ab, sigma_bb)


def tuned(mesh, sigma_sep, panel_a):
    rows_n, cols_n = mesh.shape["row"], mesh.shape["col"]
    rows = sigma_sep.shape[0] // (mesh.shape["groups"] * rows_n)
    cols = sigma_sep.shape[1] // cols_n
    return (
        rows_n == 4
        and cols_n == 4
        and panel_a.shape[1] == 4 * BLK
        and rows == BLK * PIECE * PLANS[-1][0]
        and cols % (DEPTH_STEPS * BLK) == 0
    )


def solution(mesh):
    placed = (
        P(("groups", "row"), "col"),
        P(),
        P(),
        P(("groups", "col"), "row"),
        P(("groups", "col"), "row"),
        P("groups", None),
        P(("groups", "col"), None),
        P(("groups", "col"), None),
    )
    out_placed = (
        P(("groups", "row"), "col"),
        P(("groups", "col"), None),
        P(("groups", "row"), "col"),
        P(("groups", "col"), "row"),
        P(("groups", "col"), None),
    )

    def run(sigma_sep, pattern_a, pattern_b, panel_a, panel_b, cross_b, dinv_a, dinv_b):
        body = per_device if tuned(mesh, sigma_sep, panel_a) else per_device_any
        return jax.shard_map(
            body, mesh=mesh, in_specs=placed, out_specs=out_placed, check_vma=False
        )(sigma_sep, pattern_a, pattern_b, panel_a, panel_b, cross_b, dinv_a, dinv_b)

    return run
```

```python
import functools

import jax
import jax.numpy as jnp
from jax import lax
from jax.experimental import pallas as pl
from jax.experimental.pallas import tpu as pltpu
from jax.sharding import PartitionSpec as P

BLK = 128
TOP = 32704.0
STEPS = 64.0
LN2 = 0.6931471805599453
ROUND = 1.5 * 2.0**23
TAIL = 16
VMEM = 40 * 2**20
SLOT_VMEM = 50 * 2**20

PIECE = 10
DEPTH_STEPS = 3


def code_of(values):
    top = jnp.max(jnp.abs(values), axis=0, keepdims=True)
    return jnp.ceil(jnp.log(jnp.maximum(top, 1e-30)) * (STEPS / LN2))


def scale_of(code):
    return jnp.exp(code * (LN2 / STEPS))


def coded(values, code):
    values = (values * (TOP / scale_of(code)) + ROUND) - ROUND
    return values.astype(jnp.int32).astype(jnp.int16)


def pick(table, row):
    rows = lax.broadcasted_iota(jnp.int32, table.shape, 0)
    return jnp.sum(jnp.where(rows == row, table, 0.0), axis=0, keepdims=True)


def put(table_ref, row, value):
    rows = lax.broadcasted_iota(jnp.int32, table_ref.shape, 0)
    table_ref[...] = jnp.where(rows == row, value, table_ref[...])


def decoded(message, block):
    table = message[PIECE * BLK :, :].astype(jnp.int32).astype(jnp.float32)
    values = message[block * BLK : (block + 1) * BLK, :].astype(jnp.int32).astype(jnp.float32)
    return values * (scale_of(pick(table, block)) * (1.0 / TOP))


def encode(block, values, codes, outs):
    code = code_of(values)
    values = coded(values, code)
    columns = values.shape[1] // len(outs)
    for part, out in enumerate(outs):
        out[block * BLK : (block + 1) * BLK, :] = values[:, part * columns : (part + 1) * columns]
    rows = lax.broadcasted_iota(jnp.int32, codes.shape, 0)
    return jnp.where(rows == block, code, codes)


def close(codes, outs):
    codes = codes.astype(jnp.int32).astype(jnp.int16)
    columns = codes.shape[1] // len(outs)
    for part, out in enumerate(outs):
        out[PIECE * BLK :, :] = codes[:, part * columns : (part + 1) * columns]


def split(values):
    high = values.astype(jnp.bfloat16)
    return high, (values - high.astype(jnp.float32)).astype(jnp.bfloat16)


def over_rows(left, right):
    return lax.dot_general(
        left, right, (((0,), (0,)), ((), ())), preferred_element_type=jnp.float32
    )


def dot(left, right):
    return jnp.dot(left, right, preferred_element_type=jnp.float32)


def whole(shape):
    return pl.BlockSpec(shape, lambda i, *_: (0,) * len(shape))


def params(limit=VMEM):
    return pltpu.CompilerParams(vmem_limit_bytes=limit)


FIELDS = 2 + PIECE
ENDS, PARITY, OWN = range(3)
SPOTS = 3


def here():
    return pl.BlockSpec(memory_space=pl.ANY)


def far_off():
    return pl.BlockSpec(memory_space=pltpu.HBM)


def join_kernel(spot, mask, blocks, table, mine_ref, theirs_ref, *refs):
    out_ref = refs[-1]
    even = table[spot + PARITY] == 0
    for block in range(blocks):
        rows = slice(block * BLK, (block + 1) * BLK)
        mine, theirs = mine_ref[rows, :], theirs_ref[rows, :]
        on = table[mask + pl.program_id(0) * blocks + block] == 1
        zero = jnp.zeros_like(mine)
        out_ref[rows, :BLK] = jnp.where(on, jnp.where(even, mine, theirs), zero)
        out_ref[rows, BLK:] = jnp.where(on, jnp.where(even, theirs, mine), zero)


def join(spot, mask, table, mine, theirs, after):
    rows = mine.shape[0]
    blocks = rows // (BLK * DEPTH_STEPS)
    block = pl.BlockSpec((blocks * BLK, BLK), lambda i, *_: (i, 0))
    return pl.pallas_call(
        functools.partial(join_kernel, spot, mask, blocks),
        grid_spec=pltpu.PrefetchScalarGridSpec(
            num_scalar_prefetch=1,
            grid=(DEPTH_STEPS,),
            in_specs=[block, block] + [here()] * len(after),
            out_specs=pl.BlockSpec((blocks * BLK, 2 * BLK), lambda i, *_: (i, 0)),
        ),
        out_shape=pltpu.HBM((rows, 2 * BLK), mine.dtype),
        compiler_params=params(),
        cost_estimate=pl.CostEstimate(
            flops=rows * BLK, bytes_accessed=8 * rows * BLK, transcendentals=0
        ),
        name="join",
    )(table, mine, theirs, *after)


def pass_kernel(in_ref, *refs):
    refs[-1][...] = in_ref[...]


def passed(value, after):
    block = pl.BlockSpec(value.shape, lambda i: (0,) * value.ndim)
    return pl.pallas_call(
        pass_kernel,
        grid=(1,),
        in_specs=[block] + [here()] * len(after),
        out_specs=block,
        out_shape=jax.ShapeDtypeStruct(value.shape, value.dtype),
        compiler_params=params(),
        cost_estimate=pl.CostEstimate(
            flops=value.size, bytes_accessed=4 * value.size, transcendentals=0
        ),
        name="passed",
    )(value, *after)


def slot_kernel(slot, spot, sections, gots, end, waits, aliases, table, *refs):
    refs = list(refs)

    def take(count):
        taken = refs[:count]
        del refs[:count]
        return taken

    (sigma,) = take(1)
    panels = take(len(sections))
    got_refs = take(gots)
    if end == "b":
        terms = take(4)
        cross_high, cross_low = take(2)
        rows_0, rows_1 = take(PIECE), take(PIECE)
        (total_in,) = take(1)
    take(waits + aliases)
    (msg_ref,) = take(1)
    if end == "a":
        high_ref, low_ref = take(2)
    if end:
        slice_refs = [ref.at[0] for ref in take(2)]
    if end == "b":
        (total_ref,) = take(1)
    acc, left, rhs, sems = take(4)
    valid = table[slot * FIELDS] == 1
    ends = table[spot + ENDS] == 1
    part = rhs.shape[0] // DEPTH_STEPS

    def panel_copy(panel, which):
        span = pl.ds(which * part, part)
        return pltpu.make_async_copy(panel.at[span, :], rhs.at[span, :], sems.at[which, PIECE])

    def sigma_copy(block, which):
        first = pl.multiple_of(table[slot * FIELDS + 2 + block] * BLK, BLK)
        span = pl.ds(which * part, part)
        return pltpu.make_async_copy(
            sigma.at[pl.ds(first, BLK), span],
            left.at[pl.ds(block * BLK, BLK), span],
            sems.at[which, block],
        )

    @pl.when(valid)
    def _():
        for which in range(DEPTH_STEPS):
            for section, panel in zip(sections, panels):

                @pl.when(table[slot * FIELDS + 1] == section)
                def _():
                    panel_copy(panel, which).start()

            for block in range(PIECE):
                sigma_copy(block, which).start()
        for which in range(DEPTH_STEPS):
            panel_copy(panels[0], which).wait()
            for block in range(PIECE):
                sigma_copy(block, which).wait()
            span = slice(which * part, (which + 1) * part)
            values = dot(left[:, span], rhs[span, :])
            if which:
                acc[...] += values
            else:
                acc[...] = values

    def values_of(block):
        values = acc[block * BLK : (block + 1) * BLK, :]
        for got_ref in got_refs:
            values = values + decoded(got_ref, block)
        return values

    blank = jnp.zeros((TAIL, acc.shape[1]), jnp.float32)

    @pl.when(valid & jnp.logical_not(ends))
    def _():
        codes = blank
        for block in range(PIECE):
            codes = encode(block, values_of(block), codes, [msg_ref])
        close(codes, [msg_ref])

    if end == "a":

        @pl.when(ends & jnp.logical_not(valid))
        def _():
            high_ref[...] = jnp.zeros_like(high_ref)
            low_ref[...] = jnp.zeros_like(low_ref)

        @pl.when(ends & valid)
        def _():
            codes = blank
            for block in range(PIECE):
                values = values_of(block)
                rows = slice(block * BLK, (block + 1) * BLK)
                high_ref[rows, :], low_ref[rows, :] = split(values)
                codes = encode(block, values, codes, slice_refs)
            close(codes, slice_refs)

    if end == "b":

        @pl.when(ends & jnp.logical_not(valid))
        def _():
            total_ref[...] = total_in[...]

        @pl.when(ends & valid)
        def _():
            high = jnp.concatenate([terms[0][...], terms[2][...]], axis=1)
            low = jnp.concatenate([terms[1][...], terms[3][...]], axis=1)
            acc[...] -= (
                dot(high, cross_high[...])
                + dot(high, cross_low[...])
                + dot(low, cross_high[...])
            )
            codes = blank
            for block in range(PIECE):
                values = values_of(block)
                acc[block * BLK : (block + 1) * BLK, :] = values
                codes = encode(block, values, codes, slice_refs)
            close(codes, slice_refs)
            high, low = split(acc[...])
            rows = jnp.concatenate(
                [jnp.concatenate([x[...], y[...]], axis=1) for x, y in zip(rows_0, rows_1)],
                axis=0,
            )
            total_ref[...] = total_in[...] + (over_rows(rows, high) + over_rows(rows, low))


def run_slot(slot, spot, table, sigma, panels, gots, end, extra, after, buffers, spots):
    depth = sigma.shape[1]
    width = next(iter(panels.values())).shape[1]
    rows = PIECE * BLK
    base = slot * FIELDS

    def panel_row(which):
        return lambda i, table: (table[base + 2 + which], 0)

    in_specs = [far_off()] * (1 + len(panels))
    operands = [sigma] + list(panels.values())
    message = (rows + TAIL, width)
    in_specs += [whole(message)] * len(gots)
    operands += gots
    out_specs = [whole(message)]
    out_shape = [jax.ShapeDtypeStruct(message, jnp.int16)]
    if end:
        piece, pieces, place_in, places = spots
    if end == "a":
        out_specs += [pl.BlockSpec((rows, width), lambda i, *_: (piece, 0))] * 2
        out_shape += [pltpu.HBM((pieces * rows, width), jnp.bfloat16)] * 2
    if end:
        slice_message = (1, rows + TAIL, width // 2)
        out_specs += [pl.BlockSpec(slice_message, lambda i, *_: (place_in, 0, 0))] * 2
        out_shape += [pltpu.HBM((places,) + slice_message[1:], jnp.int16)] * 2
    if end == "b":
        terms, cross, both, total = extra
        in_specs += [pl.BlockSpec((rows, width), lambda i, *_: (piece, 0))] * 4
        in_specs += [whole((2 * width, width))] * 2
        for _ in range(2):
            in_specs += [pl.BlockSpec((BLK, width), panel_row(which)) for which in range(PIECE)]
        in_specs.append(whole((2 * width, width)))
        operands += [*terms, *cross] + [both[0]] * PIECE + [both[1]] * PIECE + [total]
        out_specs.append(whole((2 * width, width)))
        out_shape.append(jax.ShapeDtypeStruct((2 * width, width), jnp.float32))
    in_specs += [here()] * len(after)
    operands += after
    aliases = {}
    count = 0
    for which, buffer in enumerate(buffers):
        if buffer is not None:
            aliases[1 + len(operands)] = 1 + which
            in_specs.append(far_off())
            operands.append(buffer)
            count += 1
    return pl.pallas_call(
        functools.partial(
            slot_kernel, slot, spot, tuple(panels), len(gots), end, len(after), count
        ),
        grid_spec=pltpu.PrefetchScalarGridSpec(
            num_scalar_prefetch=1,
            grid=(1,),
            in_specs=in_specs,
            out_specs=out_specs,
            scratch_shapes=[
                pltpu.VMEM((rows, width), jnp.float32),
                pltpu.VMEM((rows, depth), jnp.bfloat16),
                pltpu.VMEM((depth, width), jnp.bfloat16),
                pltpu.SemaphoreType.DMA((DEPTH_STEPS, PIECE + 1)),
            ],
        ),
        out_shape=out_shape,
        input_output_aliases=aliases,
        compiler_params=params(SLOT_VMEM),
        cost_estimate=pl.CostEstimate(
            flops=rows * width,
            bytes_accessed=rows * width,
            transcendentals=0,
        ),
        name="slot",
    )(table, *operands)


def square_kernel(spot, table, *refs):
    high_ref, low_ref, *panels, in_ref, out_ref = refs

    @pl.when(table[spot + ENDS] == 1)
    def _():
        @pl.when(pl.program_id(0) == 0)
        def _():
            out_ref[...] = in_ref[...]

        rows = jnp.concatenate(
            [
                jnp.concatenate([ref[...] for ref in panels[first : first + PIECE]], axis=0)
                for first in range(0, len(panels), PIECE)
            ],
            axis=1,
        )
        out_ref[...] += over_rows(high_ref[...], rows) + over_rows(low_ref[...], rows)


def square_sums(spot, order, table, first, count, terms, panels, total):
    width = terms[0].shape[1]
    rows = PIECE * BLK
    term = pl.BlockSpec((rows, width), lambda i, *_: (first + i, 0))

    def panel_row(which):
        return lambda i, table: (table[order + (first + i) * PIECE + which], 0)

    shape = (width, len(panels) * width)
    blocks = [pl.BlockSpec((BLK, width), panel_row(which)) for which in range(PIECE)]
    return pl.pallas_call(
        functools.partial(square_kernel, spot),
        grid_spec=pltpu.PrefetchScalarGridSpec(
            num_scalar_prefetch=1,
            grid=(count,),
            in_specs=[term] * 2 + blocks * len(panels) + [whole(shape)],
            out_specs=whole(shape),
        ),
        out_shape=jax.ShapeDtypeStruct(shape, jnp.float32),
        compiler_params=params(),
        cost_estimate=pl.CostEstimate(
            flops=16 * count * rows * width * width,
            bytes_accessed=12 * count * rows * width + 32 * width * width,
            transcendentals=0,
        ),
        name="square_sums",
    )(table, *terms, *[panel for panel in panels for _ in range(PIECE)], total)


def place_kernel(spot, on, order, pieces, parts, table, *refs):
    arrays = refs[: 2 * len(parts)]
    out_ref, held, sem = refs[2 * len(parts) :]
    own = table[spot + OWN]
    ends = table[spot + ENDS] == 1
    for which, (v, start, count) in enumerate(parts):
        for side, wanted in ((0, ends), (1, jnp.logical_not(ends))):

            @pl.when((own == v) & wanted)
            def _():
                source = arrays[2 * which + side]
                copy = pltpu.make_async_copy(source, held.at[pl.ds(start, count)], sem)
                copy.start()
                copy.wait()

    out_ref[...] = jnp.zeros_like(out_ref)

    @pl.loop(0, pieces)
    def _(piece):
        message = held.at[piece]
        for block in range(PIECE):
            which = piece * PIECE + block
            first = pl.multiple_of(table[order + which] * BLK, BLK)
            values = jnp.where(table[on + which] == 1, -decoded(message, block), 0.0)
            out_ref[pl.ds(first, BLK), :] = values


def place(spot, on, order, table, pieces, row_count, parts):
    message = parts[0][2].shape[1:]
    ranges = tuple((v, start, mine.shape[0]) for v, start, mine, _ in parts)
    arrays = [array for part in parts for array in part[2:]]
    return pl.pallas_call(
        functools.partial(place_kernel, spot, on, order, pieces, ranges),
        grid_spec=pltpu.PrefetchScalarGridSpec(
            num_scalar_prefetch=1,
            grid=(1,),
            in_specs=[far_off()] * len(arrays),
            out_specs=whole((row_count, BLK)),
            scratch_shapes=[
                pltpu.VMEM((pieces,) + message, jnp.int16),
                pltpu.SemaphoreType.DMA(()),
            ],
        ),
        out_shape=jax.ShapeDtypeStruct((row_count, BLK), jnp.float32),
        compiler_params=params(),
        cost_estimate=pl.CostEstimate(
            flops=20 * row_count * BLK,
            bytes_accessed=6 * row_count * BLK,
            transcendentals=0,
        ),
        name="place",
    )(table, *arrays)


def product(left, right):
    return jnp.dot(left, right, precision=lax.Precision.HIGHEST, preferred_element_type=jnp.float32)


def plan(
    pieces_a, pieces_b,
    sigma_sep, pattern_a, pattern_b, panel_a, panel_b, cross_b, dinv_a, dinv_b,
):
    rows_n = lax.axis_size("row")
    cols_n = lax.axis_size("col")
    row = lax.axis_index("row")
    col = lax.axis_index("col")
    local_rows, local_cols = sigma_sep.shape
    ratio = rows_n // cols_n
    row_blocks = local_rows // BLK
    col_blocks = local_cols // BLK
    width = panel_a.shape[1] * rows_n
    half_width = width // 2
    slices = width // BLK
    pair = row // 2
    diag = row // ratio
    on_diag = col == diag

    def at(r, c):
        return r * cols_n + c

    def home(r, v):
        return (v + 2 * (r // 2)) % slices

    ends = [(r, r // ratio) for r in range(rows_n)]
    spread = [
        [(at(r, d), at(r, home(r, v))) for r, d in ends if home(r, v) != d]
        for v in range(slices)
    ]
    own_v = (col + 2 * pair) % slices

    def path(d):
        if 2 * d >= cols_n:
            return list(range(d)) + list(range(cols_n - 1, d - 1, -1))
        return list(range(cols_n - 1, d, -1)) + list(range(d + 1))

    def send(value, pairs):
        return lax.ppermute(value, ("row", "col"), pairs)

    core_swap = [(r, r ^ 1) for r in range(rows_n)]
    chip_swap = [(r, (r + 2) % rows_n) for r in range(rows_n)]

    core_a = lax.ppermute(panel_a, "row", core_swap)
    chip_a = lax.ppermute(panel_a, "row", chip_swap)

    lengths = (pieces_a, pieces_a, pieces_b, pieces_b)
    starts = [sum(lengths[:section]) for section in range(4)]
    count = sum(lengths)
    far = cols_n - 1
    slots = count + 2 * far
    low = jnp.where(col < diag, col, diag + cols_n - 1 - col)
    high = jnp.where(col > diag, cols_n - 1 - col, cols_n - 1 - diag + col)
    delay = 2 * jnp.where(2 * diag >= cols_n, low, high)
    at_slot = jnp.arange(slots, dtype=jnp.int32) - delay
    valid = (at_slot >= 0) & (at_slot < count)
    at_slot = jnp.clip(at_slot, 0, count - 1)
    section_at = sum((at_slot >= start).astype(jnp.int32) for start in starts[1:])
    piece_at = at_slot - sum(
        jnp.where(section_at == section, start, 0) for section, start in enumerate(starts)
    )
    both = pattern_a * pattern_b
    masks = [
        lax.dynamic_slice_in_dim(pattern, index * length, length, 0)
        for index, length in ((col, col_blocks), (row, row_blocks))
        for pattern in (pattern_a, both)
    ]
    numbers = jnp.arange(row_blocks, dtype=jnp.int32)
    rank = (2 - masks[2] - masks[3]) * row_blocks + numbers
    place_of = jnp.sum((rank[None, :] < rank[:, None]).astype(jnp.int32), axis=1)
    is_at = place_of[None, :] == numbers[:, None]
    order = jnp.sum(jnp.where(is_at, numbers[None, :], 0), axis=1)
    rows_on = [jnp.sum(jnp.where(is_at, mask[None, :], 0), axis=1) for mask in masks[2:]]
    spots = piece_at[:, None] * PIECE + jnp.arange(PIECE, dtype=jnp.int32)[None, :]
    blocks = jnp.sum(
        jnp.where(spots[:, :, None] == numbers[None, None, :], order[None, None, :], 0), axis=2
    )
    left_a, left_b = (jnp.sum(mask) for mask in rows_on)
    valid &= piece_at * PIECE < jnp.where(section_at < 2, left_a, left_b)
    table = jnp.concatenate(
        [valid.astype(jnp.int32)[:, None], section_at[:, None], blocks], axis=1
    ).reshape(-1)
    spot = slots * FIELDS
    small = jnp.stack([on_diag.astype(jnp.int32), row % 2, own_v])
    table = jnp.concatenate([table, small, *masks[:2], *rows_on, order])
    cols_a = spot + SPOTS
    cols_b = cols_a + col_blocks
    rows_a = cols_b + col_blocks
    rows_b = rows_a + row_blocks
    order_at = rows_b + row_blocks

    swapped = pair % 2 == 1

    def turn(value, axis):
        return jnp.where(swapped, jnp.roll(value, half_width, axis), value)

    cross_v = turn(turn(cross_b, 0), 1)
    cross_high = lax.reduce_precision(cross_v, 8, 7)
    cross_low = (cross_v - cross_high).astype(jnp.bfloat16)
    cross_high = cross_high.astype(jnp.bfloat16)

    def inward(slot):
        pairs = []
        for r, d in ends:
            line = path(d)
            for stop, (c, after) in enumerate(zip(line, line[1:])):
                if 0 <= slot - 2 * stop < count:
                    pairs.append((at(r, c), at(r, after)))
        return pairs

    def to_columns(value):
        total = None
        for v, pairs in enumerate(spread):
            mine = value[v * BLK : (v + 1) * BLK]
            got = jnp.where(on_diag & (own_v == v), mine, send(mine, pairs))
            total = got if total is None else total + got
        return total

    def over_cores(total):
        return total + lax.ppermute(total, "row", core_swap)

    def over_row(total):
        total = over_cores(total)
        return total + lax.ppermute(total, "row", chip_swap)

    def parts_of(length, last):
        parts = []
        first = 0
        while first < length:
            size = min(3, length - first)
            if last:
                size = 1
            parts.append((first, size))
            first += size
        return parts

    batches = [parts_of(length, section == 3) for section, length in enumerate(lengths)]
    panels = {0: join(spot, cols_a, table, panel_a, core_a, [])}
    arrived = {}
    terms = {}
    slice_parts = ([], [])
    squares = [jnp.zeros((half_width, 2 * width), jnp.float32)] * 2
    totals = [jnp.zeros((width, half_width), jnp.float32)] * 2
    waiting = {}
    message = None
    end_a = 2 * far + 2 * pieces_a - 1
    middle = pieces_a // 2

    def add_squares(half, first, length):
        squares[half] = square_sums(
            spot, order_at, table, first, length, terms[half], list(panels.values()), squares[half]
        )

    for slot in range(slots):
        if slot == 2:
            later_b = passed(panel_b, [message])
            core_b = lax.ppermute(later_b, "row", core_swap)
            chip_b = lax.ppermute(later_b, "row", chip_swap)
        if slot == starts[1] - 1:
            chip_a = passed(chip_a, [message])
            both_a = lax.ppermute(chip_a, "row", core_swap)
        if slot == starts[1]:
            panels[1] = join(spot, cols_a, table, chip_a, both_a, [message])
        if slot == starts[2] - 1:
            chip_b = passed(chip_b, [message])
            both_b = lax.ppermute(chip_b, "row", core_swap)
        if slot == starts[2]:
            panels[2] = join(spot, cols_b, table, later_b, core_b, [message])
        if slot == starts[2] + 1:
            panels[3] = join(spot, cols_b, table, chip_b, both_b, [message])
        gots = arrived.pop(slot - 2, [])
        ended = slot - 2 * far
        end = ""
        if ended >= 0:
            section = sum(ended >= start for start in starts[1:])
            piece = ended - starts[section]
            half = section % 2
            end = "ab"[section // 2]
        extra = None
        buffers = []
        places = None
        if end:
            batch = next(b for b in batches[section] if b[0] <= piece < b[0] + b[1])
            places = (piece, lengths[section], piece - batch[0], batch[1])
            if end == "a":
                buffers += terms.get(half, [None, None])
            buffers += slice_bufs if piece > batch[0] else [None, None]
        if end == "b":
            cols = slice(half * half_width, (half + 1) * half_width)
            extra = (
                terms[0] + terms[1],
                (cross_high[:, cols], cross_low[:, cols]),
                (panels[2], panels[3]),
                totals[half],
            )
        first = sum(max(0, ended) >= start for start in starts[1:])
        final = sum(slot >= start for start in starts[1:])
        after = [] if message is None else [message]
        after += waiting.pop(slot, [])
        outs = run_slot(
            slot,
            spot,
            table,
            sigma_sep,
            {section: panels[section] for section in range(first, final + 1)},
            gots,
            end,
            extra,
            after,
            buffers,
            places,
        )
        message = outs[0]
        if slot < slots - 2:
            arrived[slot] = [send(message, inward(slot))]
        if end == "a":
            terms[half] = list(outs[1:3])
        if end == "b":
            totals[half] = outs[-1]
        if end:
            start = 3 if end == "a" else 1
            slice_bufs = list(outs[start : start + 2])
            if piece == batch[0] + batch[1] - 1:
                parts = slice_parts[section // 2]
                for part in range(2):
                    got = send(slice_bufs[part], spread[2 * half + part])
                    parts.append((2 * half + part, batch[0], slice_bufs[part], got))
                    waiting.setdefault(slot + (2 if section == 3 else 7), []).append(got)
        if slot == end_a - 2:
            add_squares(0, 0, middle)
        if slot == end_a - 1:
            add_squares(0, middle, pieces_a - middle)
        if slot == end_a:
            add_squares(1, 0, pieces_a)
            whole_a = jnp.concatenate(squares, axis=0)
            whole_a = jnp.concatenate([turn(whole_a[:, :width], 1), turn(whole_a[:, width:], 1)], 1)
            sums = to_columns(whole_a)
        if slot == end_a + min(4, 2 * pieces_b - 1):
            sigma_ia = place(
                spot, rows_a, order_at, table, pieces_a, local_rows, slice_parts[0]
            )
            waiting.setdefault(slot + 1, []).append(sigma_ia)
        if slot == slots - 4:
            sums = over_cores(passed(sums, [message]))
        if slot == slots - 3:
            sums = passed(sums, [message])
            sums = sums + lax.ppermute(sums, "row", chip_swap)
            waiting.setdefault(slots - 1, []).append(sums)
    sigma_aa = dinv_a + sums[:, :width]
    image_ab = product(sigma_aa, cross_b) - sums[:, width:]
    sigma_ab = -lax.dynamic_slice_in_dim(image_ab, row * BLK, BLK, 1)
    total = to_columns(turn(jnp.concatenate(totals, axis=1), 1))
    cross_own = lax.dynamic_slice_in_dim(cross_b, col * BLK, BLK, 1)
    cross_ab = dinv_b
    for shift in range(cols_n):
        pairs = [(c, (c + shift) % cols_n) for c in range(cols_n)]
        there = lax.ppermute(image_ab, "col", pairs) if shift else image_ab
        source = (col + cols_n - shift) % cols_n
        left = lax.dynamic_slice_in_dim(cross_own, source * BLK, BLK, 0)
        cross_ab = cross_ab + product(left.T, there)
    sigma_bb = cross_ab + over_row(total)
    sigma_ib = place(spot, rows_b, order_at, table, pieces_b, local_rows, slice_parts[1])
    return (sigma_ia, sigma_aa, sigma_ib, sigma_ab, sigma_bb)


PLANS = ((3, 3),)


def per_device(sigma_sep, pattern_a, pattern_b, panel_a, panel_b, cross_b, dinv_a, dinv_b):
    bands = lax.axis_size("row")
    most_a = jnp.max(jnp.sum(pattern_a.reshape(bands, -1), axis=1))
    most_b = jnp.max(jnp.sum((pattern_a * pattern_b).reshape(bands, -1), axis=1))
    fits = [(most_a <= a * PIECE) & (most_b <= b * PIECE) for a, b in PLANS]
    which = jnp.argmax(jnp.stack(fits))
    return lax.switch(
        which,
        [functools.partial(plan, a, b) for a, b in PLANS],
        sigma_sep,
        pattern_a,
        pattern_b,
        panel_a,
        panel_b,
        cross_b,
        dinv_a,
        dinv_b,
    )


def broadcast(value, axis, root):
    mine = lax.axis_index(axis) == root
    return lax.psum(jnp.where(mine, value, jnp.zeros_like(value)), axis)


def block_mask(pattern, first_row, row_count):
    blocks = (first_row + jnp.arange(row_count, dtype=jnp.int32)) // BLK
    block_ids = jnp.arange(pattern.shape[0], dtype=jnp.int32)
    matches = (blocks[:, None] == block_ids[None, :]).astype(jnp.float32)
    return product(matches, pattern.astype(jnp.float32)[:, None])


def per_device_any(sigma_sep, pattern_a, pattern_b, panel_a, panel_b, cross_b, dinv_a, dinv_b):
    row_devices = lax.axis_size("row")
    col_devices = lax.axis_size("col")
    row_index = lax.axis_index("row")
    col_index = lax.axis_index("col")
    local_rows = sigma_sep.shape[0]
    local_cols = sigma_sep.shape[1]
    panel_width = panel_a.shape[1] * row_devices
    slice_width = panel_width // col_devices
    band_width = panel_width // row_devices
    row_ratio = row_devices // col_devices
    pattern_both = pattern_a * pattern_b
    masked_a = (
        panel_a.astype(jnp.float32) * block_mask(pattern_a, col_index * local_cols, local_cols)
    ).astype(jnp.bfloat16)
    masked_b = (
        panel_b.astype(jnp.float32) * block_mask(pattern_both, col_index * local_cols, local_cols)
    ).astype(jnp.bfloat16)
    mask_a_rows = block_mask(pattern_a, row_index * local_rows, local_rows)
    mask_b_rows = block_mask(pattern_both, row_index * local_rows, local_rows)
    source_col = row_index // row_ratio
    offset = row_index % row_ratio * local_rows

    def own_rows(gathered):
        return lax.dynamic_slice_in_dim(gathered, offset, local_rows, 0)

    full_a = lax.all_gather(masked_a, "row", axis=1, tiled=True)
    rows_a = broadcast(own_rows(full_a), "col", source_col)
    rows_a32 = rows_a.astype(jnp.float32)
    partial_a = jnp.dot(sigma_sep, full_a, preferred_element_type=jnp.float32)
    image_a = lax.psum_scatter(partial_a, "col", scatter_dimension=1, tiled=True)
    sigma_ia = -mask_a_rows * image_a
    quadratic_a = lax.psum(product(image_a.T, rows_a32), "row")
    sigma_aa = dinv_a + quadratic_a
    full_b = lax.all_gather(masked_b, "row", axis=1, tiled=True)
    rows_b = broadcast(own_rows(full_b), "col", source_col)
    rows_b32 = rows_b.astype(jnp.float32)
    cross_rows = lax.dynamic_slice_in_dim(cross_b, col_index * slice_width, slice_width, 0)
    cross_cols = lax.dynamic_slice_in_dim(cross_b, row_index * band_width, band_width, 1)
    partial_b = jnp.dot(sigma_sep, full_b, preferred_element_type=jnp.float32) + product(
        sigma_ia, cross_rows
    )
    image_b = lax.psum_scatter(partial_b, "col", scatter_dimension=1, tiled=True)
    sigma_ib = -mask_b_rows * image_b
    upper_part = lax.psum_scatter(
        product(sigma_ia.T, rows_b32), "row", scatter_dimension=1, tiled=True
    )
    image_ab = upper_part + product(sigma_aa, cross_cols)
    sigma_ab = -image_ab
    first_term = product(rows_b32.T, image_b)
    second_term = product(cross_rows.T, image_ab)
    blank = jnp.zeros((panel_width, panel_width), jnp.float32)
    placed = lax.dynamic_update_slice_in_dim(blank, first_term, col_index * slice_width, 1)
    placed = placed + lax.dynamic_update_slice_in_dim(blank, second_term, row_index * band_width, 1)
    share_b = lax.psum_scatter(placed, "col", scatter_dimension=0, tiled=True)
    total_bb = lax.psum(share_b, "row")
    sigma_bb = dinv_b + total_bb
    return (sigma_ia, sigma_aa, sigma_ib, sigma_ab, sigma_bb)


def tuned(mesh, sigma_sep, panel_a):
    rows_n, cols_n = mesh.shape["row"], mesh.shape["col"]
    rows = sigma_sep.shape[0] // (mesh.shape["groups"] * rows_n)
    cols = sigma_sep.shape[1] // cols_n
    return (
        rows_n == 4
        and cols_n == 4
        and panel_a.shape[1] == 4 * BLK
        and rows == BLK * PIECE * PLANS[-1][0]
        and cols % (DEPTH_STEPS * BLK) == 0
    )


def solution(mesh):
    placed = (
        P(("groups", "row"), "col"),
        P(),
        P(),
        P(("groups", "col"), "row"),
        P(("groups", "col"), "row"),
        P("groups", None),
        P(("groups", "col"), None),
        P(("groups", "col"), None),
    )
    out_placed = (
        P(("groups", "row"), "col"),
        P(("groups", "col"), None),
        P(("groups", "row"), "col"),
        P(("groups", "col"), "row"),
        P(("groups", "col"), None),
    )

    def run(sigma_sep, pattern_a, pattern_b, panel_a, panel_b, cross_b, dinv_a, dinv_b):
        body = per_device if tuned(mesh, sigma_sep, panel_a) else per_device_any
        return jax.shard_map(
            body, mesh=mesh, in_specs=placed, out_specs=out_placed, check_vma=False
        )(sigma_sep, pattern_a, pattern_b, panel_a, panel_b, cross_b, dinv_a, dinv_b)

    return run
```
